256 devices in a mesh: dp: 8 (over y, core), rows: 32 (over z, x).
Axes of the slice: x: 4, y: 4, z: 8, core: 2. Of those that a mesh axis runs over, the one named last changes fastest.
Arguments:
- grads: bfloat16 [8, 4, 1024, 8192], P('dp', None, 'rows'), may hold values from -120 to 120
- errors: float32 [8, 4, 1024, 8192], P('dp', None, 'rows'), may hold values from -3 to 3
- q_prev: float32 [4, 8192, 64], P(None, 'rows'), may hold values from -0.0625 to 0.0625
Outputs:
- q_new: float32 [4, 8192, 64], P(None, 'rows')
- errors_new: float32 [8, 4, 1024, 8192], P('dp', None, 'rows')
The draws below stay inside these ranges and needn't reach their ends.
All inputs are finite; a program needn't handle non-finite values.
Results may differ from the reference program's by a relative error of at most 0.0003.
Values sent between devices are 32-bit elements; how exact they have to be, the bound alone decides.
A program may use at most 128 MiB of HBM per device.

```python
import math
import jax
import jax.numpy as jnp
from jax import lax

D = 8192
KV = 1024
RANK = 64
MATS = 4
GROUPS = 8


def draw_grads(key, part):
    key = jax.random.fold_in(key, 11)
    keys = jax.random.split(key, 3)
    shape = (GROUPS, MATS, KV, D)
    rise = 3.0 ** (jnp.arange(KV, dtype=jnp.float32) / (KV - 1))
    row_scale = jnp.exp(jax.random.uniform(keys[1], (GROUPS, MATS, KV, 1), jnp.float32, 0.0, math.log(10.0))) * rise[None, None, :, None]
    col_scale = jnp.exp(jax.random.uniform(keys[2], (1, MATS, 1, D), jnp.float32, 0.0, math.log(10.0)))
    group_scale = 1.0 + 2.0 * jnp.arange(GROUPS, dtype=jnp.float32) / max(GROUPS - 1, 1)
    base = jnp.clip(jax.random.normal(keys[0], shape, jnp.float32), -4.0, 4.0)
    values = base * row_scale * col_scale * group_scale[:, None, None, None] / 30.0
    return values.astype(jnp.bfloat16)


def steps_of(stream_key, dims, cuts, smallest, top_value):
    factor_of = 1.0
    for axis_at, blocks in cuts:
        heights = jax.random.uniform(jax.random.fold_in(jax.random.fold_in(stream_key, 6), axis_at), (blocks,), jnp.float32, smallest / len(cuts), top_value / len(cuts))
        factor_of = factor_of * jnp.repeat(jnp.exp(heights), dims[axis_at] // blocks).reshape((-1,) + (1,) * (len(dims) - 1 - axis_at))
    return factor_of


def normal_values(rng, extent, deviation, reach, cuts=(), held_as=jnp.bfloat16):
    factor_of = steps_of(rng, extent, cuts, -0.22, 0.18) if cuts else 1.0
    array = jax.random.normal(rng, extent, jnp.float32) * deviation * factor_of
    return jnp.minimum(jnp.maximum(array, -reach), reach).astype(held_as)


def setup_inputs(seed: int = 0) -> dict:
    key_of = jax.random.split(jax.random.key(seed), 4)
    grads = draw_grads(jax.random.fold_in(key_of[3], 71), 0)
    errors = normal_values(key_of[1], (GROUPS, MATS, KV, D), 0.5, 3.0, ((0, 8), (2, 32)), jnp.float32)
    q_prev = normal_values(key_of[2], (MATS, D, RANK), D ** -0.5, 0.0625, ((1, 32),), jnp.float32)
    return {"grads": grads, "errors": errors, "q_prev": q_prev}


def orthonormal(left):
    gram = jnp.einsum('mrk,mrl->mkl', left, left, precision=lax.Precision.HIGHEST)
    trace = jnp.trace(gram, axis1=1, axis2=2)
    eye = jnp.eye(gram.shape[1], dtype=gram.dtype)
    factor = jnp.linalg.cholesky(gram + (0.0001 * trace / gram.shape[1])[:, None, None] * eye[None])
    solved = jax.vmap(lambda low, rhs: jax.scipy.linalg.solve_triangular(low, rhs, lower=True))(factor, jnp.transpose(left, (0, 2, 1)))
    return jnp.transpose(solved, (0, 2, 1))

def reference(grads, errors, q_prev):
    merged = grads.astype(jnp.float32) + errors
    left = jnp.einsum('gmrc,mck->mrk', merged, q_prev, precision=lax.Precision.HIGHEST) / GROUPS
    ortho = orthonormal(left)
    q_new = jnp.einsum('gmrc,mrk->mck', merged, ortho, precision=lax.Precision.HIGHEST) / GROUPS
    approx = jnp.einsum('mrk,mck->mrc', ortho, q_new, precision=lax.Precision.HIGHEST)
    return (q_new, merged - approx[None])
```

```python
import jax
import jax.numpy as jnp
from jax import lax
from jax.experimental import pallas as pl
from jax.experimental.pallas import tpu as pltpu
from jax.sharding import PartitionSpec as P

MESH = pl.DeviceIdType.MESH
HIGHEST = lax.Precision.HIGHEST
NX, NY, NZ = 4, 4, 8
MATS, ROWS, RANK, GROUPS = 4, 32, 64, 8
BLOCK = 128
CHUNK = NX * 2 * BLOCK
DAMP = 0.0001

NN = (((1,), (0,)), ((), ()))
NT = (((1,), (1,)), ((), ()))

IN_ORDER = (4, 3, 5, 2, 6, 1, 7, 0)
OUT_ORDER = (0, 1, 7, 2, 6, 3, 5, 4)
PEERS = tuple((t, dx) for t in OUT_ORDER for dx in range(NX) if (t, dx) != (0, 0))


def dot(a, b, dims=NN):
    return lax.dot_general(a, b, dims, precision=HIGHEST, preferred_element_type=jnp.float32)


def inverse_factor(gram):
    n = RANK
    row = lax.broadcasted_iota(jnp.int32, (n, n), 0)
    col = lax.broadcasted_iota(jnp.int32, (n, n), 1)
    eye = jnp.where(row == col, 1.0, 0.0).astype(jnp.float32)
    trace = jnp.sum(gram * eye, axis=(0, 1), keepdims=True)
    full = jnp.concatenate([gram + (DAMP / n) * trace * eye, eye], axis=1)
    strips = [full[8 * i : 8 * i + 8] for i in range(n // 8)]
    sub = lax.broadcasted_iota(jnp.int32, (8, 2 * n), 0)
    scales = []
    for b in range(n // 8):
        live = range(b, n // 8)
        cols = {
            (i, j): jnp.broadcast_to(strips[i][:, 8 * b + j : 8 * b + j + 1], (8, 2 * n))
            for i in live
            for j in range(8)
        }
        scale = jnp.zeros((8, 2 * n), jnp.float32)
        for j in range(8):
            pivot = jnp.broadcast_to(cols[b, j][j : j + 1], (8, 2 * n))
            inv = 1.0 / pivot
            scale = jnp.where(sub == j, lax.rsqrt(pivot), scale)
            factor = {i: cols[i, j] for i in live}
            factor[b] = jnp.where(sub > j, factor[b], 0.0)
            lead = jnp.broadcast_to(strips[b][j : j + 1], (8, 2 * n)) * inv
            heads = {q: jnp.broadcast_to(cols[b, q][j : j + 1], (8, 2 * n)) * inv for q in range(j + 1, 8)}
            for i in live:
                strips[i] = strips[i] - factor[i] * lead
                for q in range(j + 1, 8):
                    cols[i, q] = cols[i, q] - factor[i] * heads[q]
        scales.append(scale)
    done = jnp.concatenate([s * c for s, c in zip(strips, scales)], axis=0)
    return done[:, n:]


def kernel(
    grads, errors, q_prev, q_out, e_out,
    g_in, e_in, q_in, merged, summed, pass_up, pass_dn, fin_up, fin_dn, mean, meant, q_all,
    acc, half_out, half_in, left, block_out, approx,
    ld_sem, q_sem, core_s, core_r, pass_s, pass_r, fin_s, fin_r, m_s, m_r, qz_s, qz_r, qx_s, qx_r,
    h_s, h_r, l_s, l_r, lc_s, lc_r, a_s, a_r, y_s, y_r, rel_s, rel_r, ac_s, ac_r, out_sem,
):
    d, r = lax.axis_index("dp"), lax.axis_index("rows")
    y, k = d // 2, d % 2
    z, x = r // NX, r % NX
    other = 1 - k
    y_up, y_dn, y_far = (y + 1) % NY, (y + 3) % NY, (y + 2) % NY
    partner = (y * 2 + other, r)
    up = (y_up * 2 + k, r)
    down = (y_dn * 2 + k, r)

    def peer(t, dx):
        return (d, ((z + t) % NZ) * NX + (x + dx) % NX)

    def zat(t):
        return (z + t) % NZ

    def xat(dx):
        return (x + dx) % NX

    sends = []

    def send(src, dst, ss, rs, to):
        copy = pltpu.make_async_remote_copy(
            src_ref=src, dst_ref=dst, send_sem=ss, recv_sem=rs, device_id=to, device_id_type=MESH
        )
        copy.start()
        sends.append(copy)
        return copy

    loads = {}
    q_load = pltpu.make_async_copy(q_prev.at[y, pl.ds(pl.multiple_of(k * BLOCK, BLOCK), BLOCK)], q_in, q_sem)
    q_load.start()
    for n, t in enumerate(IN_ORDER):
        at = pl.ds(pl.multiple_of(zat(t) * CHUNK, CHUNK), CHUNK)
        loads[n] = (
            pltpu.make_async_copy(grads.at[0, :, :, at], g_in.at[zat(t)], ld_sem.at[0, n]),
            pltpu.make_async_copy(errors.at[0, :, :, at], e_in.at[zat(t)], ld_sem.at[1, n]),
        )
        for load in loads[n]:
            load.start()

    barrier = pltpu.get_barrier_semaphore()
    for to in [partner, up, down] + [peer(t, dx) for t, dx in PEERS]:
        pl.semaphore_signal(barrier, inc=1, device_id=to, device_id_type=MESH)
    q_load.wait()
    q_all[z, x] = jnp.transpose(q_in[...])
    pl.semaphore_wait(barrier, 3 + len(PEERS))

    qz = [
        send(q_all.at[z, x], q_all.at[z, x], qz_s.at[t], qz_r.at[t], peer(t, 0)) for t in OUT_ORDER[1:]
    ]

    core, passes, finals, q_x = {}, {}, {}, []

    def four(c):
        return pl.ds(pl.multiple_of(c * NX, NX), NX)

    def merge(n):
        c = zat(IN_ORDER[n])
        for load in loads[n]:
            load.wait()

        def one(m, _):
            for j in range(2 * NX):
                cols = slice(j * BLOCK, (j + 1) * BLOCK)
                merged[m, j % 2, c * NX + j // 2] = g_in[c, m, :, cols].astype(jnp.float32) + e_in[c, m, :, cols]
            return 0

        lax.fori_loop(0, MATS, one, 0)
        core[n] = send(merged.at[:, other, four(c)], summed.at[:, four(c)], core_s.at[n], core_r.at[n], partner)

    def pair_sum(n):
        c = zat(IN_ORDER[n])
        core[n].wait_recv()

        def one(m, _):
            for j in range(NX):
                summed[m, c * NX + j] += merged[m, k, c * NX + j]
            return 0

        lax.fori_loop(0, MATS, one, 0)
        passes[n] = (
            send(summed.at[y_far, pl.ds(c * NX, 2)], pass_up.at[c], pass_s.at[0, n], pass_r.at[0, n], up),
            send(summed.at[y_far, pl.ds(c * NX + 2, 2)], pass_dn.at[c], pass_s.at[1, n], pass_r.at[1, n], down),
        )

    def pass_on(n):
        c = zat(IN_ORDER[n])
        for copy in passes[n]:
            copy.wait_recv()
        for j in range(2):
            summed[y_up, c * NX + j] += pass_up[c, j]
            summed[y_dn, c * NX + 2 + j] += pass_dn[c, j]
        finals[n] = (
            send(summed.at[y_up, four(c)], fin_up.at[c], fin_s.at[0, n], fin_r.at[0, n], up),
            send(summed.at[y_dn, four(c)], fin_dn.at[c], fin_s.at[1, n], fin_r.at[1, n], down),
        )

    mean_sent = {}

    def total(n):
        t = IN_ORDER[n]
        c = zat(t)
        for copy in finals[n]:
            copy.wait_recv()
        for j in range(NX):
            mean[c, j] = summed[y, c * NX + j] + fin_up[c, j] + fin_dn[c, j]
        for dx in range(NX):
            if (t, dx) == (0, 0):
                meant[z, x] = mean[z, x]
            else:
                mean_sent[t, dx] = send(
                    mean.at[c, xat(dx)], meant.at[z, x], m_s.at[t, dx], m_r.at[t, dx], peer(t, dx)
                )

    def spread_q():
        for copy in qz:
            copy.wait_recv()
        for dx in range(1, NX):
            q_x.append(send(q_all.at[:, x], q_all.at[:, x], qx_s.at[dx], qx_r.at[dx], peer(0, dx)))

    def project(n):
        c = zat(IN_ORDER[n])
        part = dot(mean[c, 0], q_all[c, 0], NT)
        for j in range(1, NX):
            part = part + dot(mean[c, j], q_all[c, j], NT)
        if n == 0:
            acc[...] = part
        else:
            acc[...] += part

    steps = len(IN_ORDER)
    for n in range(steps + 4):
        if n < steps:
            merge(n)
        if 0 <= n - 1 < steps:
            pair_sum(n - 1)
        if 0 <= n - 2 < steps:
            pass_on(n - 2)
        if n == 5:
            spread_q()
        if 0 <= n - 4 < steps:
            total(n - 4)
        if n == steps + 2:
            for copy in q_x:
                copy.wait_recv()
            for i in range(steps - 1):
                project(i)
    project(steps - 1)

    half_out[0] = acc[:16]
    half_out[1] = acc[16:]
    swap = send(half_out.at[other], half_in, h_s, h_r, partner)
    swap.wait_recv()
    mine = (half_out[k] + half_in[...]) * (1.0 / GROUPS)
    left[z, x, k] = jnp.concatenate([mine[:8], mine[8:]], axis=1)
    spread = [
        send(left.at[z, x, k], left.at[z, x, k], l_s.at[t, dx], l_r.at[t, dx], peer(t, dx)) for t, dx in PEERS
    ]
    for copy in spread:
        copy.wait_recv()
    cross = send(left.at[:, :, k], left.at[:, :, k], lc_s, lc_r, partner)
    for copy in mean_sent.values():
        copy.wait_recv()
    cross.wait_recv()

    parts = [left[:, :, i].reshape(NZ * NX * 8, BLOCK) for i in range(2)]
    turned = [jnp.transpose(p) for p in parts]
    square = dot(turned[0], parts[0]) + dot(turned[1], parts[1])
    gram = square[:RANK, :RANK] + square[RANK:, RANK:]
    inv = inverse_factor(gram)

    def rows_of(i, j):
        return pl.ds(16 * i + 8 * j, 8)

    prod = [
        sum(dot(turned[i], meant[:, :, rows_of(i, j)].reshape(NZ * NX * 8, BLOCK)) for i in range(2))
        for j in range(2)
    ]
    proj = prod[0][:RANK] + prod[1][RANK:]
    q_mine = dot(inv, proj) * (1.0 / GROUPS)
    solved = dot(jnp.transpose(inv), q_mine)
    zero = jnp.zeros((RANK, BLOCK), jnp.float32)
    wide = [jnp.concatenate([solved, zero], axis=0), jnp.concatenate([zero, solved], axis=0)]
    approx[k, y, 32] = q_mine[:32]
    approx[k, y, 33] = q_mine[32:]
    for i in range(2):
        for j in range(2):
            block_out[:, :, rows_of(i, j)] = dot(parts[i], wide[j]).reshape(NZ, NX, 8, BLOCK)

    blocks = {
        (t, dx): send(
            block_out.at[zat(t), xat(dx)], approx.at[k, y, r], a_s.at[t, dx], a_r.at[t, dx], peer(t, dx)
        )
        for t, dx in PEERS
    }
    approx[k, y, r] = block_out[z, x]

    direct, relay, crossed, outs = {}, {}, {}, []

    def places(n):
        if n == steps:
            return pl.ds(32, 2), pl.ds(32, 1), pl.ds(33, 1)
        c = (z + NZ - OUT_ORDER[n]) % NZ
        return four(c), pl.ds(c * NX, 2), pl.ds(c * NX + 2, 2)

    def share(n):
        if n < steps:
            for dx in range(NX):
                if (OUT_ORDER[n], dx) != (0, 0):
                    blocks[OUT_ORDER[n], dx].wait_recv()
        at = places(n)[0]
        here = approx.at[k, y, at]
        direct[n] = (
            send(here, here, y_s.at[0, n], y_r.at[0, n], up),
            send(here, here, y_s.at[1, n], y_r.at[1, n], down),
        )

    def pass_along(n):
        _, first, second = places(n)
        for copy in direct[n]:
            copy.wait_recv()
        from_dn, from_up = approx.at[k, y_dn, first], approx.at[k, y_up, second]
        relay[n] = (
            send(from_dn, from_dn, rel_s.at[0, n], rel_r.at[0, n], up),
            send(from_up, from_up, rel_s.at[1, n], rel_r.at[1, n], down),
        )

    def over(n):
        for copy in relay[n]:
            copy.wait_recv()
        here = approx.at[k, :, places(n)[0]]
        crossed[n] = send(here, here, ac_s.at[n], ac_r.at[n], partner)

    def finish(n):
        crossed[n].wait_recv()
        if n == steps:
            for m in range(MATS):
                for h in range(2):
                    q_out[m, h * BLOCK : (h + 1) * BLOCK] = jnp.transpose(
                        approx[h, m, 32:34].reshape(RANK, BLOCK)
                    )
            return
        c = (z + NZ - OUT_ORDER[n]) % NZ

        def one(m, _):
            for j in range(2 * NX):
                b = c * NX + j // 2
                e_in[c, m, :, j * BLOCK : (j + 1) * BLOCK] = merged[m, j % 2, b] - approx[j % 2, m, b]
            return 0

        lax.fori_loop(0, MATS, one, 0)
        at = pl.ds(pl.multiple_of(c * CHUNK, CHUNK), CHUNK)
        out = pltpu.make_async_copy(e_in.at[c], e_out.at[0, :, :, at], out_sem.at[n])
        out.start()
        outs.append(out)

    order = [steps] + list(range(steps))
    for n in range(len(order) + 3):
        if n < len(order):
            share(order[n])
        if 0 <= n - 1 < len(order):
            pass_along(order[n - 1])
        if 0 <= n - 2 < len(order):
            over(order[n - 2])
        if 0 <= n - 3 < len(order):
            finish(order[n - 3])

    for copy in sends:
        copy.wait_send()
    for out in outs:
        out.wait()


def body(grads, errors, q_prev):
    f32 = jnp.float32
    dma = pltpu.SemaphoreType.DMA
    blocks = NZ * NX
    q_new, errors_new = pl.pallas_call(
        kernel,
        out_shape=(
            jax.ShapeDtypeStruct((MATS, 2 * BLOCK, RANK), f32),
            jax.ShapeDtypeStruct(errors.shape, f32),
        ),
        in_specs=[pl.BlockSpec(memory_space=pl.ANY)] * 3,
        out_specs=(pl.BlockSpec(memory_space=pltpu.VMEM), pl.BlockSpec(memory_space=pl.ANY)),
        scratch_shapes=[
            pltpu.VMEM((NZ, MATS, ROWS, CHUNK), grads.dtype),
            pltpu.VMEM((NZ, MATS, ROWS, CHUNK), f32),
            pltpu.VMEM((BLOCK, RANK), f32),
            pltpu.VMEM((MATS, 2, blocks, ROWS, BLOCK), f32),
            pltpu.VMEM((MATS, blocks, ROWS, BLOCK), f32),
            pltpu.VMEM((NZ, 2, ROWS, BLOCK), f32),
            pltpu.VMEM((NZ, 2, ROWS, BLOCK), f32),
            pltpu.VMEM((NZ, NX, ROWS, BLOCK), f32),
            pltpu.VMEM((NZ, NX, ROWS, BLOCK), f32),
            pltpu.VMEM((NZ, NX, ROWS, BLOCK), f32),
            pltpu.VMEM((NZ, NX, ROWS, BLOCK), f32),
            pltpu.VMEM((NZ, NX, RANK, BLOCK), f32),
            pltpu.VMEM((ROWS, RANK), f32),
            pltpu.VMEM((2, ROWS // 2, RANK), f32),
            pltpu.VMEM((ROWS // 2, RANK), f32),
            pltpu.VMEM((NZ, NX, 2, 8, BLOCK), f32),
            pltpu.VMEM((NZ, NX, ROWS, BLOCK), f32),
            pltpu.VMEM((2, MATS, blocks + 2, ROWS, BLOCK), f32),
            dma((2, 8)), dma,
            dma((8,)), dma((8,)),
            dma((2, 8)), dma((2, 8)),
            dma((2, 8)), dma((2, 8)),
            dma((NZ, NX)), dma((NZ, NX)),
            dma((NZ,)), dma((NZ,)),
            dma((NX,)), dma((NX,)),
            dma, dma,
            dma((NZ, NX)), dma((NZ, NX)),
            dma, dma,
            dma((NZ, NX)), dma((NZ, NX)),
            dma((2, 9)), dma((2, 9)),
            dma((2, 9)), dma((2, 9)),
            dma((9,)), dma((9,)),
            dma((8,)),
        ],
        name="powersgd",
        compiler_params=pltpu.CompilerParams(
            collective_id=0, has_side_effects=True, vmem_limit_bytes=48 << 20
        ),
    )(grads, errors, q_prev)
    return q_new, errors_new


def solution(mesh):
    return jax.shard_map(
        body,
        mesh=mesh,
        in_specs=(P("dp", None, "rows", None), P("dp", None, "rows", None), P(None, "rows", None)),
        out_specs=(P(None, "rows", None), P("dp", None, "rows", None)),
        check_vma=False,
    )
```

```python
import jax
import jax.numpy as jnp
from jax import lax
from jax.experimental import pallas as pl
from jax.experimental.pallas import tpu as pltpu
from jax.sharding import PartitionSpec as P

MESH = pl.DeviceIdType.MESH
HIGHEST = lax.Precision.HIGHEST
NX, NY, NZ = 4, 4, 8
MATS, ROWS, RANK, GROUPS = 4, 32, 64, 8
BLOCK = 128
CHUNK = NX * 2 * BLOCK
DAMP = 0.0001

NN = (((1,), (0,)), ((), ()))
NT = (((1,), (1,)), ((), ()))

IN_ORDER = (4, 3, 5, 2, 6, 1, 7, 0)
OUT_ORDER = (0, 1, 7, 2, 6, 3, 5, 4)
ONWARD = {0: (1, 7), 1: (2,), 2: (3,), 3: (4,), 4: (), 5: (), 6: (5,), 7: (6,)}
PEERS = tuple((t, dx) for t in OUT_ORDER for dx in range(NX) if (t, dx) != (0, 0))


def dot(a, b, dims=NN):
    return lax.dot_general(a, b, dims, precision=HIGHEST, preferred_element_type=jnp.float32)


def inverse_factor(gram):
    n = RANK
    row = lax.broadcasted_iota(jnp.int32, (n, n), 0)
    col = lax.broadcasted_iota(jnp.int32, (n, n), 1)
    eye = jnp.where(row == col, 1.0, 0.0).astype(jnp.float32)
    trace = jnp.sum(gram * eye, axis=(0, 1), keepdims=True)
    full = jnp.concatenate([gram + (DAMP / n) * trace * eye, eye], axis=1)
    strips = [full[8 * i : 8 * i + 8] for i in range(n // 8)]
    sub = lax.broadcasted_iota(jnp.int32, (8, 2 * n), 0)
    scales = []
    for b in range(n // 8):
        live = range(b, n // 8)
        cols = {
            (i, j): jnp.broadcast_to(strips[i][:, 8 * b + j : 8 * b + j + 1], (8, 2 * n))
            for i in live
            for j in range(8)
        }
        scale = jnp.zeros((8, 2 * n), jnp.float32)
        for j in range(8):
            pivot = jnp.broadcast_to(cols[b, j][j : j + 1], (8, 2 * n))
            inv = 1.0 / pivot
            scale = jnp.where(sub == j, lax.rsqrt(pivot), scale)
            factor = {i: cols[i, j] for i in live}
            factor[b] = jnp.where(sub > j, factor[b], 0.0)
            lead = jnp.broadcast_to(strips[b][j : j + 1], (8, 2 * n)) * inv
            heads = {q: jnp.broadcast_to(cols[b, q][j : j + 1], (8, 2 * n)) * inv for q in range(j + 1, 8)}
            for i in live:
                strips[i] = strips[i] - factor[i] * lead
                for q in range(j + 1, 8):
                    cols[i, q] = cols[i, q] - factor[i] * heads[q]
        scales.append(scale)
    done = jnp.concatenate([s * c for s, c in zip(strips, scales)], axis=0)
    return done[:, n:]


def kernel(
    grads, errors, q_prev, q_out, e_out,
    g_in, e_in, merged, summed, pass_up, pass_dn, fin_up, fin_dn, mean, meant, q_all,
    acc, half_out, half_in, left, v_all, block_out, approx,
    ld_sem, q_sem, core_s, core_r, pass_s, pass_r, fin_s, fin_r, m_s, m_r, qz_s, qz_r, qx_s, qx_r,
    h_s, h_r, v_s, v_r, l_s, l_r, lc_s, lc_r, a_s, a_r, y_s, y_r, rel_s, rel_r, ac_s, ac_r,
):
    d, r = lax.axis_index("dp"), lax.axis_index("rows")
    y, k = d // 2, d % 2
    z, x = r // NX, r % NX
    other = 1 - k
    y_up, y_dn, y_far = (y + 1) % NY, (y + 3) % NY, (y + 2) % NY
    partner = (y * 2 + other, r)
    up = (y_up * 2 + k, r)
    down = (y_dn * 2 + k, r)

    def peer(t, dx):
        return (d, ((z + t) % NZ) * NX + (x + dx) % NX)

    def zat(t):
        return (z + t) % NZ

    def xat(dx):
        return (x + dx) % NX

    def ring(buf, ss, rs, copies, t):
        here = buf((z + NZ - t) % NZ)
        for u in ONWARD[t]:
            copies[u] = send(here, here, ss.at[u], rs.at[u], peer(1 if u <= 4 else 7, 0))

    sends = []

    def send(src, dst, ss, rs, to):
        copy = pltpu.make_async_remote_copy(
            src_ref=src, dst_ref=dst, send_sem=ss, recv_sem=rs, device_id=to, device_id_type=MESH
        )
        copy.start()
        sends.append(copy)
        return copy

    loads = {}
    q_load = pltpu.make_async_copy(
        q_prev.at[y, :, pl.ds(pl.multiple_of(k * BLOCK, BLOCK), BLOCK)], q_all.at[z, x], q_sem
    )
    q_load.start()
    for n, t in enumerate(IN_ORDER):
        at = pl.ds(pl.multiple_of(zat(t) * CHUNK, CHUNK), CHUNK)
        loads[n] = (
            pltpu.make_async_copy(grads.at[0, :, :, at], g_in.at[zat(t)], ld_sem.at[0, n]),
            pltpu.make_async_copy(errors.at[0, :, :, at], e_in.at[zat(t)], ld_sem.at[1, n]),
        )
        for load in loads[n]:
            load.start()

    barrier = pltpu.get_barrier_semaphore()
    for to in [partner, up, down] + [peer(t, dx) for t, dx in PEERS]:
        pl.semaphore_signal(barrier, inc=1, device_id=to, device_id_type=MESH)
    core, passes, finals, q_z, q_x = {}, {}, {}, {}, {}

    def four(c):
        return pl.ds(pl.multiple_of(c * NX, NX), NX)

    def merge(n):
        c = zat(IN_ORDER[n])
        for load in loads[n]:
            load.wait()

        def one(m, _):
            for j in range(2 * NX):
                cols = slice(j * BLOCK, (j + 1) * BLOCK)
                merged[m, j % 2, c * NX + j // 2] = g_in[c, m, :, cols].astype(jnp.float32) + e_in[c, m, :, cols]
            return 0

        lax.fori_loop(0, MATS, one, 0)

    def swap_cores(n):
        c = zat(IN_ORDER[n])
        core[n] = send(merged.at[:, other, four(c)], summed.at[:, four(c)], core_s.at[n], core_r.at[n], partner)

    def pair_sum(n):
        c = zat(IN_ORDER[n])
        core[n].wait_recv()

        def one(m, _):
            for j in range(NX):
                summed[m, c * NX + j] += merged[m, k, c * NX + j]
            return 0

        lax.fori_loop(0, MATS, one, 0)
        passes[n] = (
            send(summed.at[y_far, pl.ds(c * NX, 2)], pass_up.at[c], pass_s.at[0, n], pass_r.at[0, n], up),
            send(summed.at[y_far, pl.ds(c * NX + 2, 2)], pass_dn.at[c], pass_s.at[1, n], pass_r.at[1, n], down),
        )

    def pass_on(n):
        c = zat(IN_ORDER[n])
        for copy in passes[n]:
            copy.wait_recv()
        for j in range(2):
            summed[y_up, c * NX + j] += pass_up[c, j]
            summed[y_dn, c * NX + 2 + j] += pass_dn[c, j]
        finals[n] = (
            send(summed.at[y_up, four(c)], fin_up.at[c], fin_s.at[0, n], fin_r.at[0, n], up),
            send(summed.at[y_dn, four(c)], fin_dn.at[c], fin_s.at[1, n], fin_r.at[1, n], down),
        )

    mean_sent = {}

    def total(n):
        t = IN_ORDER[n]
        c = zat(t)
        for copy in finals[n]:
            copy.wait_recv()
        for j in range(NX):
            mean[c, j] = summed[y, c * NX + j] + fin_up[c, j] + fin_dn[c, j]
        for dx in range(NX):
            if (t, dx) == (0, 0):
                meant[z, x] = mean[z, x]
            else:
                mean_sent[t, dx] = send(
                    mean.at[c, xat(dx)], meant.at[z, x], m_s.at[t, dx], m_r.at[t, dx], peer(t, dx)
                )

    def spread_q(t):
        if t > 0:
            q_z[t].wait_recv()
        ring(lambda c: q_all.at[c, x], qz_s, qz_r, q_z, t)
        here = q_all.at[(z + NZ - t) % NZ, x]
        for dx in (1, 3):
            q_x[t, dx] = send(here, here, qx_s.at[t, dx], qx_r.at[t, dx], peer(0, dx))

    def relay_q(t):
        for dx in (1, 3):
            q_x[t, dx].wait_recv()
        dx = 1 if t < 4 else 3
        here = q_all.at[(z + NZ - t) % NZ, xat(NX - dx)]
        q_x[t, 2] = send(here, here, qx_s.at[t, 2], qx_r.at[t, 2], peer(0, dx))

    def project(n):
        c = zat(IN_ORDER[n])
        part = dot(mean[c, 0], q_all[c, 0], NT)
        for j in range(1, NX):
            part = part + dot(mean[c, j], q_all[c, j], NT)
        if n == 0:
            acc[...] = part
        else:
            acc[...] += part

    steps = len(IN_ORDER)
    for n in range(steps):
        merge(n)
    q_load.wait()
    pl.semaphore_wait(barrier, 3 + len(PEERS))

    for n in range(steps):
        swap_cores(n)
    spread_q(0)
    plan = [
        (pair_sum, 0), (pair_sum, 1), (pair_sum, 2), (pair_sum, 3), (spread_q, 1), (spread_q, 7),
        (pair_sum, 4), (pair_sum, 5), (pair_sum, 6), (pair_sum, 7), (relay_q, 0), (pass_on, 0), (pass_on, 1),
        (spread_q, 2), (spread_q, 6), (relay_q, 1), (relay_q, 7), (pass_on, 2), (pass_on, 3), (total, 0),
        (spread_q, 3), (spread_q, 5), (relay_q, 2), (relay_q, 6), (pass_on, 4), (total, 1), (pass_on, 5),
        (total, 2), (spread_q, 4), (relay_q, 3), (relay_q, 5), (pass_on, 6), (total, 3), (pass_on, 7),
        (total, 4), (relay_q, 4), (total, 5), (total, 6),
    ]
    for step, n in plan:
        step(n)
    for t in range(NZ):
        q_x[t, 2].wait_recv()
    for n in range(steps - 1):
        project(n)
    total(steps - 1)
    project(steps - 1)

    half_out[0] = acc[:16]
    half_out[1] = acc[16:]
    swap = send(half_out.at[other], half_in, h_s, h_r, partner)
    swap.wait_recv()
    mine = (half_out[k] + half_in[...]) * (1.0 / GROUPS)
    left[z, x, k] = jnp.concatenate([mine[:8], mine[8:]], axis=1)
    spread = [
        send(left.at[z, x, k], left.at[z, x, k], l_s.at[t, dx], l_r.at[t, dx], peer(t, dx)) for t, dx in PEERS
    ]
    for copy in spread:
        copy.wait_recv()
    cross = send(left.at[:, :, k], left.at[:, :, k], lc_s, lc_r, partner)
    for copy in mean_sent.values():
        copy.wait_recv()
    cross.wait_recv()

    parts = [left[:, :, i].reshape(NZ * NX * 8, BLOCK) for i in range(2)]
    turned = [jnp.transpose(p) for p in parts]
    square = dot(turned[0], parts[0]) + dot(turned[1], parts[1])
    gram = square[:RANK, :RANK] + square[RANK:, RANK:]
    inv = inverse_factor(gram)

    def rows_of(i, j):
        return pl.ds(16 * i + 8 * j, 8)

    prod = [
        sum(dot(turned[i], meant[:, :, rows_of(i, j)].reshape(NZ * NX * 8, BLOCK)) for i in range(2))
        for j in range(2)
    ]
    proj = prod[0][:RANK] + prod[1][RANK:]
    q_mine = dot(inv, proj) * (1.0 / GROUPS)
    solved = dot(jnp.transpose(inv), q_mine)
    v_all[z] = solved
    v_sent = {}
    zero = jnp.zeros((RANK, BLOCK), jnp.float32)
    rows = left[z].reshape(NX * 2 * 8, BLOCK)
    approx[k, y, 32] = q_mine[:32]
    approx[k, y, 33] = q_mine[32:]

    def expand(n):
        t = OUT_ORDER[n]
        c = (z + NZ - t) % NZ
        if n > 0:
            v_sent[t].wait_recv()
        ring(lambda c: v_all.at[c], v_s, v_r, v_sent, t)
        v = v_all[c]
        for j in range(2):
            wide = jnp.concatenate([v, zero] if j == 0 else [zero, v], axis=0)
            got = dot(rows, wide).reshape(NX, 2, 8, BLOCK)
            for i in range(2):
                block_out[c, :, rows_of(i, j)] = got[:, i]
        for dx in range(1, NX):
            blocks[n, dx] = send(
                block_out.at[c, xat(dx)], approx.at[k, y, c * NX + x], a_s.at[t, dx], a_r.at[t, dx], peer(0, dx)
            )
        approx[k, y, c * NX + x] = block_out[c, x]

    blocks, direct, relay, crossed = {}, {}, {}, {}

    def places(n):
        if n == steps:
            return pl.ds(32, 2), pl.ds(32, 1), pl.ds(33, 1)
        c = (z + NZ - OUT_ORDER[n]) % NZ
        return four(c), pl.ds(c * NX, 2), pl.ds(c * NX + 2, 2)

    def share(n):
        if n < steps:
            for dx in range(1, NX):
                blocks[n, dx].wait_recv()
        at = places(n)[0]
        here = approx.at[k, y, at]
        direct[n] = (
            send(here, here, y_s.at[0, n], y_r.at[0, n], up),
            send(here, here, y_s.at[1, n], y_r.at[1, n], down),
        )

    def pass_along(n):
        _, first, second = places(n)
        for copy in direct[n]:
            copy.wait_recv()
        from_dn, from_up = approx.at[k, y_dn, first], approx.at[k, y_up, second]
        relay[n] = (
            send(from_dn, from_dn, rel_s.at[0, n], rel_r.at[0, n], up),
            send(from_up, from_up, rel_s.at[1, n], rel_r.at[1, n], down),
        )

    def over(n):
        for copy in relay[n]:
            copy.wait_recv()
        here = approx.at[k, :, places(n)[0]]
        crossed[n] = send(here, here, ac_s.at[n], ac_r.at[n], partner)

    def finish(n):
        crossed[n].wait_recv()
        if n == steps:
            for m in range(MATS):
                for h in range(2):
                    q_out[m, :, h * BLOCK : (h + 1) * BLOCK] = approx[h, m, 32:34].reshape(RANK, BLOCK)
            return
        c = (z + NZ - OUT_ORDER[n]) % NZ

        def one(m, _):
            for j in range(2 * NX):
                b = c * NX + j // 2
                at = pl.ds(pl.multiple_of(c * CHUNK + j * BLOCK, BLOCK), BLOCK)
                e_out[0, m, :, at] = merged[m, j % 2, b] - approx[j % 2, m, b]
            return 0

        lax.fori_loop(0, MATS, one, 0)

    Q = steps
    plan = [
        (expand, 0), (share, Q), (share, 0), (expand, 1), (expand, 2), (share, 1), (share, 2), (pass_along, Q),
        (pass_along, 0), (expand, 3), (expand, 4), (share, 3), (share, 4), (pass_along, 1), (pass_along, 2),
        (over, Q), (over, 0), (expand, 5), (expand, 6), (share, 5), (share, 6), (pass_along, 3), (pass_along, 4),
        (over, 1), (over, 2), (expand, 7), (share, 7), (finish, Q), (finish, 0), (pass_along, 5), (pass_along, 6),
        (over, 3), (over, 4), (finish, 1), (finish, 2), (pass_along, 7), (over, 5), (over, 6), (finish, 3),
        (finish, 4), (over, 7), (finish, 5), (finish, 6), (finish, 7),
    ]
    for step, n in plan:
        step(n)

    for copy in sends:
        copy.wait_send()


def body(grads, errors, q_prev):
    f32 = jnp.float32
    dma = pltpu.SemaphoreType.DMA
    blocks = NZ * NX
    q_new, errors_new = pl.pallas_call(
        kernel,
        out_shape=(
            jax.ShapeDtypeStruct((MATS, RANK, 2 * BLOCK), f32),
            jax.ShapeDtypeStruct(errors.shape, f32),
        ),
        in_specs=[pl.BlockSpec(memory_space=pltpu.HBM)] * 3,
        out_specs=(pl.BlockSpec(memory_space=pltpu.VMEM), pl.BlockSpec(memory_space=pltpu.VMEM)),
        scratch_shapes=[
            pltpu.VMEM((NZ, MATS, ROWS, CHUNK), grads.dtype),
            pltpu.VMEM((NZ, MATS, ROWS, CHUNK), f32),
            pltpu.VMEM((MATS, 2, blocks, ROWS, BLOCK), f32),
            pltpu.VMEM((MATS, blocks, ROWS, BLOCK), f32),
            pltpu.VMEM((NZ, 2, ROWS, BLOCK), f32),
            pltpu.VMEM((NZ, 2, ROWS, BLOCK), f32),
            pltpu.VMEM((NZ, NX, ROWS, BLOCK), f32),
            pltpu.VMEM((NZ, NX, ROWS, BLOCK), f32),
            pltpu.VMEM((NZ, NX, ROWS, BLOCK), f32),
            pltpu.VMEM((NZ, NX, ROWS, BLOCK), f32),
            pltpu.VMEM((NZ, NX, RANK, BLOCK), f32),
            pltpu.VMEM((ROWS, RANK), f32),
            pltpu.VMEM((2, ROWS // 2, RANK), f32),
            pltpu.VMEM((ROWS // 2, RANK), f32),
            pltpu.VMEM((NZ, NX, 2, 8, BLOCK), f32),
            pltpu.VMEM((NZ, RANK, BLOCK), f32),
            pltpu.VMEM((NZ, NX, ROWS, BLOCK), f32),
            pltpu.VMEM((2, MATS, blocks + 2, ROWS, BLOCK), f32),
            dma((2, 8)), dma,
            dma((8,)), dma((8,)),
            dma((2, 8)), dma((2, 8)),
            dma((2, 8)), dma((2, 8)),
            dma((NZ, NX)), dma((NZ, NX)),
            dma((NZ,)), dma((NZ,)),
            dma((NZ, NX)), dma((NZ, NX)),
            dma, dma,
            dma((NZ,)), dma((NZ,)),
            dma((NZ, NX)), dma((NZ, NX)),
            dma, dma,
            dma((NZ, NX)), dma((NZ, NX)),
            dma((2, 9)), dma((2, 9)),
            dma((2, 9)), dma((2, 9)),
            dma((9,)), dma((9,)),
        ],
        name="powersgd",
        compiler_params=pltpu.CompilerParams(
            collective_id=0, has_side_effects=True, vmem_limit_bytes=46 << 20
        ),
    )(grads, errors, jnp.swapaxes(q_prev, 1, 2))
    return jnp.swapaxes(q_new, 1, 2), errors_new


def solution(mesh):
    return jax.shard_map(
        body,
        mesh=mesh,
        in_specs=(P("dp", None, "rows", None), P("dp", None, "rows", None), P(None, "rows", None)),
        out_specs=(P(None, "rows", None), P("dp", None, "rows", None)),
        check_vma=False,
    )
```

```python
import jax
import jax.numpy as jnp
from jax import lax
from jax.experimental import pallas as pl
from jax.experimental.pallas import tpu as pltpu
from jax.sharding import PartitionSpec as P

MESH = pl.DeviceIdType.MESH
HIGHEST = lax.Precision.HIGHEST
NX, NY, NZ = 4, 4, 8
MATS, ROWS, RANK, GROUPS = 4, 32, 64, 8
BLOCK = 128
CHUNK = NX * 2 * BLOCK
DAMP = 0.0001

NN = (((1,), (0,)), ((), ()))
NT = (((1,), (1,)), ((), ()))

ORDER = (0, 1, 7, 2, 6, 3, 5, 4)
ONWARD = {0: (1, 7), 1: (2,), 2: (3,), 3: (4,), 4: (), 5: (), 6: (5,), 7: (6,)}
ONWARD_FAR = {2: (3,), 3: (4,), 6: (5,)}
PEERS = tuple((t, dx) for t in ORDER for dx in range(NX) if (t, dx) != (0, 0))


def dot(a, b, dims=NN):
    return lax.dot_general(a, b, dims, precision=HIGHEST, preferred_element_type=jnp.float32)


def inverse_factor(gram):
    n = RANK
    row = lax.broadcasted_iota(jnp.int32, (n, n), 0)
    col = lax.broadcasted_iota(jnp.int32, (n, n), 1)
    eye = jnp.where(row == col, 1.0, 0.0).astype(jnp.float32)
    trace = jnp.sum(gram * eye, axis=(0, 1), keepdims=True)
    full = jnp.concatenate([gram + (DAMP / n) * trace * eye, eye], axis=1)
    strips = [full[8 * i : 8 * i + 8] for i in range(n // 8)]
    sub = lax.broadcasted_iota(jnp.int32, (8, 2 * n), 0)
    scales = []
    for b in range(n // 8):
        live = range(b, n // 8)
        cols = {
            (i, j): jnp.broadcast_to(strips[i][:, 8 * b + j : 8 * b + j + 1], (8, 2 * n))
            for i in live
            for j in range(8)
        }
        scale = jnp.zeros((8, 2 * n), jnp.float32)
        for j in range(8):
            pivot = jnp.broadcast_to(cols[b, j][j : j + 1], (8, 2 * n))
            inv = 1.0 / pivot
            scale = jnp.where(sub == j, lax.rsqrt(pivot), scale)
            factor = {i: cols[i, j] for i in live}
            factor[b] = jnp.where(sub > j, factor[b], 0.0)
            lead = jnp.broadcast_to(strips[b][j : j + 1], (8, 2 * n)) * inv
            heads = {q: jnp.broadcast_to(cols[b, q][j : j + 1], (8, 2 * n)) * inv for q in range(j + 1, 8)}
            for i in live:
                strips[i] = strips[i] - factor[i] * lead
                for q in range(j + 1, 8):
                    cols[i, q] = cols[i, q] - factor[i] * heads[q]
        scales.append(scale)
    done = jnp.concatenate([s * c for s, c in zip(strips, scales)], axis=0)
    return done[:, n:]


def kernel(
    grads, errors, q_prev, q_out, e_out,
    g_in, e_in, merged, summed, pass_up, pass_dn, fin_up, fin_dn, mean, meant, q_all,
    acc, half_out, half_in, left, v_all, block_out, approx,
    ld_sem, q_sem, core_s, core_r, pass_s, pass_r, fin_s, fin_r, m_s, m_r, qz_s, qz_r, qx_s, qx_r,
    h_s, h_r, v_s, v_r, l_s, l_r, lc_s, lc_r, a_s, a_r, y_s, y_r, rel_s, rel_r, ac_s, ac_r,
):
    d, r = lax.axis_index("dp"), lax.axis_index("rows")
    y, k = d // 2, d % 2
    z, x = r // NX, r % NX
    other = 1 - k
    y_up, y_dn, y_far = (y + 1) % NY, (y + 3) % NY, (y + 2) % NY
    partner = (y * 2 + other, r)
    up = (y_up * 2 + k, r)
    down = (y_dn * 2 + k, r)

    def peer(t, dx):
        return (d, ((z + t) % NZ) * NX + (x + dx) % NX)

    def zat(t):
        return (z + t) % NZ

    def xat(dx):
        return (x + dx) % NX

    def ring(buf, ss, rs, copies, t, onward=ONWARD):
        here = buf((z + NZ - t) % NZ)
        for u in onward.get(t, ()):
            copies[u] = send(here, here, ss.at[u], rs.at[u], peer(1 if u <= 4 else 7, 0))

    sends = []

    def flush():
        while sends:
            sends.pop(0).wait_send()

    def send(src, dst, ss, rs, to):
        copy = pltpu.make_async_remote_copy(
            src_ref=src, dst_ref=dst, send_sem=ss, recv_sem=rs, device_id=to, device_id_type=MESH
        )
        copy.start()
        sends.append(copy)
        return copy

    loads = {}
    q_load = pltpu.make_async_copy(
        q_prev.at[y, :, pl.ds(pl.multiple_of(k * BLOCK, BLOCK), BLOCK)], q_all.at[z, x], q_sem
    )
    q_load.start()
    for n, t in enumerate(ORDER):
        at = pl.ds(pl.multiple_of(zat(t) * CHUNK, CHUNK), CHUNK)
        loads[n] = (
            pltpu.make_async_copy(grads.at[0, :, :, at], g_in.at[zat(t)], ld_sem.at[0, n]),
            pltpu.make_async_copy(errors.at[0, :, :, at], e_in.at[zat(t)], ld_sem.at[1, n]),
        )
        for load in loads[n]:
            load.start()

    barrier = pltpu.get_barrier_semaphore()
    near = [partner, up, down, peer(1, 0), peer(7, 0), peer(0, 1), peer(0, 3)]
    for to in near:
        pl.semaphore_signal(barrier, inc=1, device_id=to, device_id_type=MESH)
    core, passes, finals, q_z, q_x = {}, {}, {}, {}, {}

    def four(c):
        return pl.ds(pl.multiple_of(c * NX, NX), NX)

    def merge(n):
        c = zat(ORDER[n])
        for load in loads[n]:
            load.wait()

        def one(m, _):
            for j in range(2 * NX):
                cols = slice(j * BLOCK, (j + 1) * BLOCK)
                merged[m, j % 2, c * NX + j // 2] = g_in[c, m, :, cols].astype(jnp.float32) + e_in[c, m, :, cols]
            return 0

        lax.fori_loop(0, MATS, one, 0)

    def swap_cores(n):
        c = zat(ORDER[n])
        core[n] = send(merged.at[:, other, four(c)], summed.at[:, four(c)], core_s.at[n], core_r.at[n], partner)

    def pair_sum(n):
        c = zat(ORDER[n])
        core[n].wait_recv()

        def one(m, _):
            for j in range(NX):
                summed[m, c * NX + j] += merged[m, k, c * NX + j]
            return 0

        lax.fori_loop(0, MATS, one, 0)
        passes[n] = (
            send(summed.at[y_far, pl.ds(c * NX, 2)], pass_up.at[c], pass_s.at[0, n], pass_r.at[0, n], up),
            send(summed.at[y_far, pl.ds(c * NX + 2, 2)], pass_dn.at[c], pass_s.at[1, n], pass_r.at[1, n], down),
        )

    def pass_on(n):
        c = zat(ORDER[n])
        for copy in passes[n]:
            copy.wait_recv()
        for j in range(2):
            summed[y_up, c * NX + j] += pass_up[c, j]
            summed[y_dn, c * NX + 2 + j] += pass_dn[c, j]
        finals[n] = (
            send(summed.at[y_up, four(c)], fin_up.at[c], fin_s.at[0, n], fin_r.at[0, n], up),
            send(summed.at[y_dn, four(c)], fin_dn.at[c], fin_s.at[1, n], fin_r.at[1, n], down),
        )

    mean_sent = {}

    def total(n):
        c = zat(ORDER[n])
        for copy in finals[n]:
            copy.wait_recv()
        for j in range(NX):
            mean[c, j] = summed[y, c * NX + j] + fin_up[c, j] + fin_dn[c, j]

    def scatter(n):
        t = ORDER[n]
        c = zat(t)
        for dx in range(NX):
            if (t, dx) == (0, 0):
                meant[z, x] = mean[z, x]
            else:
                mean_sent[t, dx] = send(
                    mean.at[c, xat(dx)], meant.at[z, x], m_s.at[t, dx], m_r.at[t, dx], peer(t, dx)
                )

    def spread_q(t):
        if t > 0:
            q_z[t].wait_recv()
        ring(lambda c: q_all.at[c, x], qz_s, qz_r, q_z, t)
        here = q_all.at[(z + NZ - t) % NZ, x]
        for dx in (1, 3):
            q_x[t, dx] = send(here, here, qx_s.at[t, dx], qx_r.at[t, dx], peer(0, dx))

    def relay_q(t):
        for dx in (1, 3):
            q_x[t, dx].wait_recv()
        dx = 1 if t < 4 else 3
        here = q_all.at[(z + NZ - t) % NZ, xat(NX - dx)]
        q_x[t, 2] = send(here, here, qx_s.at[t, 2], qx_r.at[t, 2], peer(0, dx))

    def project(n):
        t = ORDER[n]
        c = zat(t)
        q_x[(NZ - t) % NZ, 2].wait_recv()
        part = dot(mean[c, 0], q_all[c, 0], NT)
        for j in range(1, NX):
            part = part + dot(mean[c, j], q_all[c, j], NT)
        if n == 0:
            acc[...] = part
        else:
            acc[...] += part

    steps = len(ORDER)
    merge(0)
    pl.semaphore_wait(barrier, len(near))
    swap_cores(0)
    q_load.wait()
    plan = [
        (merge, 1), (swap_cores, 1), (spread_q, 0), (merge, 2), (swap_cores, 2), (pair_sum, 0), (merge, 3),
        (swap_cores, 3), (pair_sum, 1), (merge, 4), (swap_cores, 4), (pair_sum, 2), (merge, 5), (swap_cores, 5),
        (pair_sum, 3), (merge, 6), (swap_cores, 6), (pair_sum, 4), (merge, 7), (swap_cores, 7), (pair_sum, 5),
        (pair_sum, 6), (pair_sum, 7), (pass_on, 0), (spread_q, 1), (spread_q, 7), (pass_on, 1), (pass_on, 2),
        (relay_q, 0), (pass_on, 3), (spread_q, 2), (spread_q, 6), (pass_on, 4), (relay_q, 1), (relay_q, 7),
        (pass_on, 5), (pass_on, 6), (pass_on, 7), (total, 0), (project, 0), (scatter, 0), (spread_q, 3),
        (spread_q, 5), (total, 1), (project, 1), (scatter, 1), (relay_q, 2), (relay_q, 6), (total, 2),
        (project, 2), (scatter, 2), (spread_q, 4), (total, 3), (project, 3), (scatter, 3), (relay_q, 3),
        (relay_q, 5), (total, 4), (project, 4), (scatter, 4), (relay_q, 4), (total, 5), (project, 5), (scatter, 5),
        (total, 6), (project, 6), (scatter, 6), (total, 7), (project, 7),
    ]
    for step, n in plan:
        step(n)

    half_out[0] = acc[:16]
    half_out[1] = acc[16:]
    swap = send(half_out.at[other], half_in, h_s, h_r, partner)
    swap.wait_recv()
    mine = (half_out[k] + half_in[...]) * (1.0 / GROUPS)
    left[z, x, k] = jnp.concatenate([mine[:8], mine[8:]], axis=1)
    spread = [
        send(left.at[z, x, k], left.at[z, x, k], l_s.at[t, dx], l_r.at[t, dx], peer(t, dx))
        for t, dx in reversed(PEERS)
    ]
    scatter(steps - 1)
    flush()
    for copy in spread:
        copy.wait_recv()
    cross = send(left.at[:, :, k], left.at[:, :, k], lc_s, lc_r, partner)
    for copy in mean_sent.values():
        copy.wait_recv()

    def rows_of(i, j):
        return pl.ds(pl.multiple_of(16 * i + 8 * j, 8), 8)

    def products(i):
        part = left[:, :, i].reshape(NZ * NX * 8, BLOCK)
        turned = jnp.transpose(part)
        prod = [dot(turned, meant[:, :, rows_of(i, j)].reshape(NZ * NX * 8, BLOCK)) for j in range(2)]
        return prod[0][:RANK] + prod[1][RANK:], dot(turned, part)

    proj, square = products(k)
    cross.wait_recv()
    more = products(other)
    square = square + more[1]
    v_all[z] = proj + more[0]
    v_sent = {t: send(v_all.at[z], v_all.at[z], v_s.at[t], v_r.at[t], peer(t, 0)) for t in (1, 7, 2, 6)}
    inv = inverse_factor(square[:RANK, :RANK] + square[RANK:, RANK:])
    rows = left[z].reshape(NX * 2 * 8, BLOCK)
    ortho = jnp.concatenate([dot(rows[:, :RANK], inv, NT), dot(rows[:, RANK:], inv, NT)], axis=0)
    blocks, direct, relay, crossed = {}, {}, {}, {}
    early = list(sends)
    sends.clear()

    def expand(n):
        t = ORDER[n]
        c = (z + NZ - t) % NZ
        if n > 0:
            v_sent[t].wait_recv()
        ring(lambda c: v_all.at[c], v_s, v_r, v_sent, t, ONWARD_FAR)
        q_part = dot(inv, v_all[c]) * (1.0 / GROUPS)
        if n == 0:
            approx[k, y, 32] = q_part[:32]
            approx[k, y, 33] = q_part[32:]
        got = dot(ortho, q_part).reshape(2, NX, 2, 8, BLOCK)
        for i in range(2):
            for j in range(2):
                block_out[c, :, rows_of(i, j)] = got[j, :, i]
        for dx in range(1, NX):
            blocks[n, dx] = send(
                block_out.at[c, xat(dx)], approx.at[k, y, c * NX + x], a_s.at[t, dx], a_r.at[t, dx], peer(0, dx)
            )
        approx[k, y, c * NX + x] = block_out[c, x]


    def places(n):
        if n == steps:
            return pl.ds(32, 2), pl.ds(32, 1), pl.ds(33, 1)
        c = (z + NZ - ORDER[n]) % NZ
        return four(c), pl.ds(c * NX, 2), pl.ds(c * NX + 2, 2)

    def share(n):
        if n < steps:
            for dx in range(1, NX):
                blocks[n, dx].wait_recv()
        at = places(n)[0]
        here = approx.at[k, y, at]
        direct[n] = (
            send(here, here, y_s.at[0, n], y_r.at[0, n], up),
            send(here, here, y_s.at[1, n], y_r.at[1, n], down),
        )

    def cross_over(n, m, slot):
        here = approx.at[k, m, places(n)[0]]
        crossed[n, slot] = send(here, here, ac_s.at[slot, n], ac_r.at[slot, n], partner)

    def pass_along(n):
        _, first, second = places(n)
        for copy in direct[n]:
            copy.wait_recv()
        from_dn, from_up = approx.at[k, y_dn, first], approx.at[k, y_up, second]
        relay[n] = (
            send(from_dn, from_dn, rel_s.at[0, n], rel_r.at[0, n], up),
            send(from_up, from_up, rel_s.at[1, n], rel_r.at[1, n], down),
        )
        for slot, m in enumerate((y, y_up, y_dn)):
            cross_over(n, m, slot)

    def over(n):
        for copy in relay[n]:
            copy.wait_recv()
        cross_over(n, y_far, 3)

    def tidy(n):
        for copy in early:
            copy.wait_send()
        early.clear()
        for _ in range(n):
            sends.pop(0).wait_send()

    def finish(n):
        for slot in range(MATS):
            crossed[n, slot].wait_recv()
        if n == steps:
            for m in range(MATS):
                for h in range(2):
                    q_out[m, :, h * BLOCK : (h + 1) * BLOCK] = approx[h, m, 32:34].reshape(RANK, BLOCK)
            return
        c = (z + NZ - ORDER[n]) % NZ

        def one(m, _):
            for j in range(2 * NX):
                b = c * NX + j // 2
                at = pl.ds(pl.multiple_of(c * CHUNK + j * BLOCK, BLOCK), BLOCK)
                e_out[0, m, :, at] = merged[m, j % 2, b] - approx[j % 2, m, b]
            return 0

        lax.fori_loop(0, MATS, one, 0)

    Q = steps
    plan = [
        (expand, 0), (share, Q), (expand, 1), (expand, 2), (share, 0), (expand, 3), (expand, 4), (share, 1),
        (share, 2), (pass_along, Q), (pass_along, 0), (expand, 5), (expand, 6), (share, 3), (share, 4),
        (pass_along, 1), (pass_along, 2), (expand, 7), (over, Q), (over, 0), (share, 5), (share, 6),
        (pass_along, 3), (pass_along, 4), (over, 1), (over, 2), (share, 7), (finish, Q), (finish, 0),
        (pass_along, 5), (pass_along, 6), (over, 3), (over, 4), (finish, 1), (finish, 2), (pass_along, 7),
        (over, 5), (over, 6), (finish, 3), (finish, 4), (tidy, 80), (over, 7), (finish, 5), (finish, 6), (finish, 7),
    ]
    for step, n in plan:
        step(n)
    flush()


def body(grads, errors, q_prev):
    f32 = jnp.float32
    dma = pltpu.SemaphoreType.DMA
    blocks = NZ * NX
    q_new, errors_new = pl.pallas_call(
        kernel,
        out_shape=(
            jax.ShapeDtypeStruct((MATS, RANK, 2 * BLOCK), f32),
            jax.ShapeDtypeStruct(errors.shape, f32),
        ),
        in_specs=[pl.BlockSpec(memory_space=pltpu.HBM)] * 3,
        out_specs=(pl.BlockSpec(memory_space=pltpu.VMEM), pl.BlockSpec(memory_space=pltpu.VMEM)),
        scratch_shapes=[
            pltpu.VMEM((NZ, MATS, ROWS, CHUNK), grads.dtype),
            pltpu.VMEM((NZ, MATS, ROWS, CHUNK), f32),
            pltpu.VMEM((MATS, 2, blocks, ROWS, BLOCK), f32),
            pltpu.VMEM((MATS, blocks, ROWS, BLOCK), f32),
            pltpu.VMEM((NZ, 2, ROWS, BLOCK), f32),
            pltpu.VMEM((NZ, 2, ROWS, BLOCK), f32),
            pltpu.VMEM((NZ, NX, ROWS, BLOCK), f32),
            pltpu.VMEM((NZ, NX, ROWS, BLOCK), f32),
            pltpu.VMEM((NZ, NX, ROWS, BLOCK), f32),
            pltpu.VMEM((NZ, NX, ROWS, BLOCK), f32),
            pltpu.VMEM((NZ, NX, RANK, BLOCK), f32),
            pltpu.VMEM((ROWS, RANK), f32),
            pltpu.VMEM((2, ROWS // 2, RANK), f32),
            pltpu.VMEM((ROWS // 2, RANK), f32),
            pltpu.VMEM((NZ, NX, 2, 8, BLOCK), f32),
            pltpu.VMEM((NZ, RANK, BLOCK), f32),
            pltpu.VMEM((NZ, NX, ROWS, BLOCK), f32),
            pltpu.VMEM((2, MATS, blocks + 2, ROWS, BLOCK), f32),
            dma((2, 8)), dma,
            dma((8,)), dma((8,)),
            dma((2, 8)), dma((2, 8)),
            dma((2, 8)), dma((2, 8)),
            dma((NZ, NX)), dma((NZ, NX)),
            dma((NZ,)), dma((NZ,)),
            dma((NZ, NX)), dma((NZ, NX)),
            dma, dma,
            dma((NZ,)), dma((NZ,)),
            dma((NZ, NX)), dma((NZ, NX)),
            dma, dma,
            dma((NZ, NX)), dma((NZ, NX)),
            dma((2, 9)), dma((2, 9)),
            dma((2, 9)), dma((2, 9)),
            dma((MATS, 9)), dma((MATS, 9)),
        ],
        name="powersgd",
        compiler_params=pltpu.CompilerParams(
            collective_id=0, has_side_effects=True, vmem_limit_bytes=46 << 20
        ),
    )(*(pltpu.with_memory_space_constraint(v, pltpu.HBM) for v in (grads, errors, jnp.swapaxes(q_prev, 1, 2))))
    return jnp.swapaxes(q_new, 1, 2), errors_new


def solution(mesh):
    return jax.shard_map(
        body,
        mesh=mesh,
        in_specs=(P("dp", None, "rows", None), P("dp", None, "rows", None), P(None, "rows", None)),
        out_specs=(P(None, "rows", None), P("dp", None, "rows", None)),
        check_vma=False,
    )
```

```python
import jax
import jax.numpy as jnp
from jax import lax
from jax.experimental import pallas as pl
from jax.experimental.pallas import tpu as pltpu
from jax.sharding import PartitionSpec as P

MESH = pl.DeviceIdType.MESH
HIGHEST = lax.Precision.HIGHEST
NX, NY, NZ = 4, 4, 8
MATS, ROWS, RANK, GROUPS = 4, 32, 64, 8
BLOCK = 128
CHUNK = NX * 2 * BLOCK
DAMP = 0.0001

NN = (((1,), (0,)), ((), ()))
NT = (((1,), (1,)), ((), ()))

ORDER = (0, 1, 7, 2, 6, 3, 5, 4)
IN_ORDER = (4, 3, 5, 2, 6, 1, 7, 0)
ONWARD = {0: (1, 7), 1: (2,), 2: (3,), 3: (4,), 4: (), 5: (), 6: (5,), 7: (6,)}
ONWARD_FAR = {2: (3,), 3: (4,), 6: (5,)}
PEERS = tuple((t, dx) for t in ORDER for dx in range(NX) if (t, dx) != (0, 0))


def dot(a, b, dims=NN):
    return lax.dot_general(a, b, dims, precision=HIGHEST, preferred_element_type=jnp.float32)


def inverse_factor(gram):
    n = RANK
    row = lax.broadcasted_iota(jnp.int32, (n, n), 0)
    col = lax.broadcasted_iota(jnp.int32, (n, n), 1)
    eye = jnp.where(row == col, 1.0, 0.0).astype(jnp.float32)
    trace = jnp.sum(gram * eye, axis=(0, 1), keepdims=True)
    full = jnp.concatenate([gram + (DAMP / n) * trace * eye, eye], axis=1)
    strips = [full[8 * i : 8 * i + 8] for i in range(n // 8)]
    sub = lax.broadcasted_iota(jnp.int32, (8, 2 * n), 0)
    scales = []
    for b in range(n // 8):
        live = range(b, n // 8)
        cols = {
            (i, j): jnp.broadcast_to(strips[i][:, 8 * b + j : 8 * b + j + 1], (8, 2 * n))
            for i in live
            for j in range(8)
        }
        scale = jnp.zeros((8, 2 * n), jnp.float32)
        for j in range(8):
            pivot = jnp.broadcast_to(cols[b, j][j : j + 1], (8, 2 * n))
            inv = 1.0 / pivot
            scale = jnp.where(sub == j, lax.rsqrt(pivot), scale)
            factor = {i: cols[i, j] for i in live}
            factor[b] = jnp.where(sub > j, factor[b], 0.0)
            lead = jnp.broadcast_to(strips[b][j : j + 1], (8, 2 * n)) * inv
            heads = {q: jnp.broadcast_to(cols[b, q][j : j + 1], (8, 2 * n)) * inv for q in range(j + 1, 8)}
            for i in live:
                strips[i] = strips[i] - factor[i] * lead
                for q in range(j + 1, 8):
                    cols[i, q] = cols[i, q] - factor[i] * heads[q]
        scales.append(scale)
    done = jnp.concatenate([s * c for s, c in zip(strips, scales)], axis=0)
    return done[:, n:]


def kernel(
    grads, errors, q_prev, q_out, e_out,
    g_in, e_in, merged, summed, pass_up, pass_dn, fin_up, fin_dn, mean, meant, q_all,
    acc, half_out, half_in, left, v_all, block_out, approx,
    ld_sem, q_sem, core_s, core_r, pass_s, pass_r, fin_s, fin_r, m_s, m_r, qz_s, qz_r, qx_s, qx_r, x_known, z_known,
    h_s, h_r, v_s, v_r, l_s, l_r, lc_s, lc_r, a_s, a_r, y_s, y_r, rel_s, rel_r, ac_s, ac_r,
):
    d, r = lax.axis_index("dp"), lax.axis_index("rows")
    y, k = d // 2, d % 2
    z, x = r // NX, r % NX
    other = 1 - k
    y_up, y_dn, y_far = (y + 1) % NY, (y + 3) % NY, (y + 2) % NY
    partner = (y * 2 + other, r)
    up = (y_up * 2 + k, r)
    down = (y_dn * 2 + k, r)

    def peer(t, dx):
        return (d, ((z + t) % NZ) * NX + (x + dx) % NX)

    def zat(t):
        return (z + t) % NZ

    def xat(dx):
        return (x + dx) % NX

    def ring(buf, ss, rs, copies, t, onward=ONWARD):
        here = buf((z + NZ - t) % NZ)
        for u in onward.get(t, ()):
            copies[u] = send(here, here, ss.at[u], rs.at[u], peer(1 if u <= 4 else 7, 0))

    sends = []

    def flush():
        while sends:
            sends.pop(0).wait_send()

    def send(src, dst, ss, rs, to):
        copy = pltpu.make_async_remote_copy(
            src_ref=src, dst_ref=dst, send_sem=ss, recv_sem=rs, device_id=to, device_id_type=MESH
        )
        copy.start()
        sends.append(copy)
        return copy

    loads = {}
    q_load = pltpu.make_async_copy(
        q_prev.at[y, :, pl.ds(pl.multiple_of(k * BLOCK, BLOCK), BLOCK)], q_all.at[z, x], q_sem
    )
    q_load.start()
    for n, t in enumerate(IN_ORDER):
        at = pl.ds(pl.multiple_of(zat(t) * CHUNK, CHUNK), CHUNK)
        loads[n] = (
            pltpu.make_async_copy(grads.at[0, :, :, at], g_in.at[zat(t)], ld_sem.at[0, n]),
            pltpu.make_async_copy(errors.at[0, :, :, at], e_in.at[zat(t)], ld_sem.at[1, n]),
        )
        for load in loads[n]:
            load.start()

    barrier = pltpu.get_barrier_semaphore()
    near = [partner, up, down, peer(1, 0), peer(7, 0), peer(0, 1), peer(0, 3)]
    for to in near:
        pl.semaphore_signal(barrier, inc=1, device_id=to, device_id_type=MESH)
    core, passes, finals, q_z, q_x = {}, {}, {}, {}, {}

    def four(c):
        return pl.ds(pl.multiple_of(c * NX, NX), NX)

    def merge(n):
        c = zat(IN_ORDER[n])
        for load in loads[n]:
            load.wait()

        def one(m, _):
            for j in range(2 * NX):
                cols = slice(j * BLOCK, (j + 1) * BLOCK)
                merged[m, j % 2, c * NX + j // 2] = g_in[c, m, :, cols].astype(jnp.float32) + e_in[c, m, :, cols]
            return 0

        lax.fori_loop(0, MATS, one, 0)

    def swap_cores(n):
        c = zat(IN_ORDER[n])
        core[n] = send(merged.at[:, other, four(c)], summed.at[:, four(c)], core_s.at[n], core_r.at[n], partner)

    def pair_sum(n):
        c = zat(IN_ORDER[n])
        core[n].wait_recv()

        def one(m, _):
            for j in range(NX):
                summed[m, c * NX + j] += merged[m, k, c * NX + j]
            return 0

        lax.fori_loop(0, MATS, one, 0)
        passes[n] = (
            send(summed.at[y_far, pl.ds(c * NX, 2)], pass_up.at[c], pass_s.at[0, n], pass_r.at[0, n], up),
            send(summed.at[y_far, pl.ds(c * NX + 2, 2)], pass_dn.at[c], pass_s.at[1, n], pass_r.at[1, n], down),
        )

    def pass_on(n):
        c = zat(IN_ORDER[n])
        for copy in passes[n]:
            copy.wait_recv()
        for j in range(2):
            summed[y_up, c * NX + j] += pass_up[c, j]
            summed[y_dn, c * NX + 2 + j] += pass_dn[c, j]
        finals[n] = (
            send(summed.at[y_up, four(c)], fin_up.at[c], fin_s.at[0, n], fin_r.at[0, n], up),
            send(summed.at[y_dn, four(c)], fin_dn.at[c], fin_s.at[1, n], fin_r.at[1, n], down),
        )

    mean_sent = {}

    def total(n):
        c = zat(IN_ORDER[n])
        for copy in finals[n]:
            copy.wait_recv()
        for j in range(NX):
            mean[c, j] = summed[y, c * NX + j] + fin_up[c, j] + fin_dn[c, j]

    def scatter(n):
        t = IN_ORDER[n]
        c = zat(t)
        for dx in range(NX):
            if (t, dx) == (0, 0):
                meant[z, x] = mean[z, x]
            else:
                mean_sent[t, dx] = send(
                    mean.at[c, xat(dx)], meant.at[z, x], m_s.at[t, dx], m_r.at[t, dx], peer(t, dx)
                )

    def hello(n):
        if n == 1:
            pl.semaphore_wait(x_known, 1)
        elif n == 5:
            pl.semaphore_wait(z_known.at[0, 3], 1)
        elif n > 1:
            for way in range(2):
                pl.semaphore_wait(z_known.at[way, n - 2], 1)
        if n == 0:
            pl.semaphore_signal(x_known, inc=1, device_id=peer(0, 1), device_id_type=MESH)
        elif n < 5:
            for way in range(2 if n < 4 else 1):
                to = peer((1, 7)[way], 0)
                pl.semaphore_signal(z_known.at[way, n - 1], inc=1, device_id=to, device_id_type=MESH)

    def spread_q(t):
        if t > 0:
            q_z[t].wait_recv()
        ring(lambda c: q_all.at[c, x], qz_s, qz_r, q_z, t)
        here = q_all.at[(z + NZ - t) % NZ, x]
        for dx in (1, 3):
            q_x[t, dx] = send(here, here, qx_s.at[t, dx], qx_r.at[t, dx], peer(0, dx))

    def relay_q(t):
        for dx in (1, 3):
            q_x[t, dx].wait_recv()
        dx = 1 if t < 4 else 3
        here = q_all.at[(z + NZ - t) % NZ, xat(NX - dx)]
        q_x[t, 2] = send(here, here, qx_s.at[t, 2], qx_r.at[t, 2], peer(0, dx))

    def project(n):
        t = IN_ORDER[n]
        c = zat(t)
        q_x[(NZ - t) % NZ, 2].wait_recv()
        part = dot(mean[c, 0], q_all[c, 0], NT)
        for j in range(1, NX):
            part = part + dot(mean[c, j], q_all[c, j], NT)
        acc[...] += part

    steps = len(IN_ORDER)
    merge(0)
    pl.semaphore_wait(barrier, len(near))
    swap_cores(0)
    q_load.wait()
    acc[...] = jnp.zeros_like(acc)
    plan = [
        (hello, 0), (merge, 1), (swap_cores, 1), (spread_q, 0), (merge, 2), (swap_cores, 2), (pair_sum, 0),
        (hello, 1), (merge, 3), (swap_cores, 3), (pair_sum, 1), (merge, 4), (swap_cores, 4), (pair_sum, 2),
        (merge, 5), (swap_cores, 5), (hello, 2), (pair_sum, 3), (merge, 6), (swap_cores, 6), (pair_sum, 4),
        (merge, 7), (swap_cores, 7), (pair_sum, 5), (hello, 3), (pair_sum, 6), (pair_sum, 7), (pass_on, 0),
        (spread_q, 1), (spread_q, 7), (pass_on, 1), (hello, 4), (pass_on, 2), (relay_q, 0), (pass_on, 3),
        (spread_q, 2), (spread_q, 6), (pass_on, 4), (relay_q, 1), (relay_q, 7), (hello, 5), (pass_on, 5),
        (pass_on, 6), (pass_on, 7), (total, 0), (scatter, 0), (spread_q, 3), (spread_q, 5), (total, 1),
        (scatter, 1), (relay_q, 2), (relay_q, 6), (total, 2), (scatter, 2), (spread_q, 4), (total, 3),
        (scatter, 3), (relay_q, 3), (relay_q, 5), (total, 4), (scatter, 4), (project, 4), (project, 3),
        (relay_q, 4), (total, 5), (scatter, 5), (project, 5), (project, 1), (project, 2), (total, 6),
        (scatter, 6), (project, 6), (project, 0), (total, 7), (scatter, 7), (project, 7),
    ]
    for step, n in plan:
        step(n)

    half_out[0] = acc[:16]
    half_out[1] = acc[16:]
    swap = send(half_out.at[other], half_in, h_s, h_r, partner)
    swap.wait_recv()
    mine = (half_out[k] + half_in[...]) * (1.0 / GROUPS)
    left[z, x, k] = jnp.concatenate([mine[:8], mine[8:]], axis=1)
    spread = [
        send(left.at[z, x, k], left.at[z, x, k], l_s.at[t, dx], l_r.at[t, dx], peer(t, dx))
        for t, dx in reversed(PEERS)
    ]
    flush()
    for copy in spread:
        copy.wait_recv()
    cross = send(left.at[:, :, k], left.at[:, :, k], lc_s, lc_r, partner)
    for copy in mean_sent.values():
        copy.wait_recv()

    def rows_of(i, j):
        return pl.ds(pl.multiple_of(16 * i + 8 * j, 8), 8)

    def products(i):
        part = left[:, :, i].reshape(NZ * NX * 8, BLOCK)
        turned = jnp.transpose(part)
        prod = [dot(turned, meant[:, :, rows_of(i, j)].reshape(NZ * NX * 8, BLOCK)) for j in range(2)]
        return prod[0][:RANK] + prod[1][RANK:], dot(turned, part)

    proj, square = products(k)
    cross.wait_recv()
    more = products(other)
    square = square + more[1]
    v_all[z] = proj + more[0]
    v_sent = {t: send(v_all.at[z], v_all.at[z], v_s.at[t], v_r.at[t], peer(t, 0)) for t in (1, 7, 2, 6)}
    inv = inverse_factor(square[:RANK, :RANK] + square[RANK:, RANK:])
    rows = left[z].reshape(NX * 2 * 8, BLOCK)
    ortho = jnp.concatenate([dot(rows[:, :RANK], inv, NT), dot(rows[:, RANK:], inv, NT)], axis=0)
    blocks, direct, relay, crossed = {}, {}, {}, {}
    early = list(sends)
    sends.clear()

    def expand(n):
        t = ORDER[n]
        c = (z + NZ - t) % NZ
        if n > 0:
            v_sent[t].wait_recv()
        ring(lambda c: v_all.at[c], v_s, v_r, v_sent, t, ONWARD_FAR)
        q_part = dot(inv, v_all[c]) * (1.0 / GROUPS)
        if n == 0:
            approx[k, y, 32] = q_part[:32]
            approx[k, y, 33] = q_part[32:]
        got = dot(ortho, q_part).reshape(2, NX, 2, 8, BLOCK)
        for i in range(2):
            for j in range(2):
                block_out[c, :, rows_of(i, j)] = got[j, :, i]
        for dx in range(1, NX):
            blocks[n, dx] = send(
                block_out.at[c, xat(dx)], approx.at[k, y, c * NX + x], a_s.at[t, dx], a_r.at[t, dx], peer(0, dx)
            )
        approx[k, y, c * NX + x] = block_out[c, x]


    def places(n):
        if n == steps:
            return pl.ds(32, 2), pl.ds(32, 1), pl.ds(33, 1)
        c = (z + NZ - ORDER[n]) % NZ
        return four(c), pl.ds(c * NX, 2), pl.ds(c * NX + 2, 2)

    def share(n):
        if n < steps:
            for dx in range(1, NX):
                blocks[n, dx].wait_recv()
        at = places(n)[0]
        here = approx.at[k, y, at]
        direct[n] = (
            send(here, here, y_s.at[0, n], y_r.at[0, n], up),
            send(here, here, y_s.at[1, n], y_r.at[1, n], down),
        )

    def cross_over(n, m, slot):
        here = approx.at[k, m, places(n)[0]]
        crossed[n, slot] = send(here, here, ac_s.at[slot, n], ac_r.at[slot, n], partner)

    def pass_along(n):
        _, first, second = places(n)
        for copy in direct[n]:
            copy.wait_recv()
        from_dn, from_up = approx.at[k, y_dn, first], approx.at[k, y_up, second]
        relay[n] = (
            send(from_dn, from_dn, rel_s.at[0, n], rel_r.at[0, n], up),
            send(from_up, from_up, rel_s.at[1, n], rel_r.at[1, n], down),
        )
        for slot, m in enumerate((y, y_up, y_dn)):
            cross_over(n, m, slot)

    def over(n):
        for copy in relay[n]:
            copy.wait_recv()
        cross_over(n, y_far, 3)

    def tidy(n):
        for copy in early:
            copy.wait_send()
        early.clear()
        for _ in range(n):
            sends.pop(0).wait_send()

    def finish(n):
        for slot in range(MATS):
            crossed[n, slot].wait_recv()
        if n == steps:
            for m in range(MATS):
                for h in range(2):
                    q_out[m, :, h * BLOCK : (h + 1) * BLOCK] = approx[h, m, 32:34].reshape(RANK, BLOCK)
            return
        c = (z + NZ - ORDER[n]) % NZ

        def one(m, _):
            for j in range(2 * NX):
                b = c * NX + j // 2
                at = pl.ds(pl.multiple_of(c * CHUNK + j * BLOCK, BLOCK), BLOCK)
                e_out[0, m, :, at] = merged[m, j % 2, b] - approx[j % 2, m, b]
            return 0

        lax.fori_loop(0, MATS, one, 0)

    Q = steps
    plan = [
        (expand, 0), (share, Q), (expand, 1), (expand, 2), (share, 0), (expand, 3), (expand, 4), (share, 1),
        (share, 2), (pass_along, Q), (pass_along, 0), (expand, 5), (expand, 6), (share, 3), (share, 4),
        (pass_along, 1), (pass_along, 2), (expand, 7), (over, Q), (over, 0), (share, 5), (share, 6),
        (pass_along, 3), (pass_along, 4), (over, 1), (over, 2), (share, 7), (finish, Q), (finish, 0),
        (pass_along, 5), (pass_along, 6), (over, 3), (over, 4), (finish, 1), (finish, 2), (pass_along, 7),
        (over, 5), (over, 6), (finish, 3), (finish, 4), (tidy, 80), (over, 7), (finish, 5), (finish, 6), (finish, 7),
    ]
    for step, n in plan:
        step(n)
    flush()


def store(e_in, q_in, e_out, q_out, sem):
    copies = [pltpu.make_async_copy(e_in.at[:, m], e_out.at[:, m], sem.at[m]) for m in range(MATS)]
    copies.append(pltpu.make_async_copy(q_in, q_out, sem.at[MATS]))
    for copy in copies:
        copy.start()
    for copy in copies:
        copy.wait()


def body(grads, errors, q_prev):
    f32 = jnp.float32
    dma = pltpu.SemaphoreType.DMA
    blocks = NZ * NX
    q_new, errors_new = pl.pallas_call(
        kernel,
        out_shape=(
            jax.ShapeDtypeStruct((MATS, RANK, 2 * BLOCK), f32),
            jax.ShapeDtypeStruct(errors.shape, f32),
        ),
        in_specs=[pl.BlockSpec(memory_space=pltpu.HBM)] * 3,
        out_specs=(pl.BlockSpec(memory_space=pltpu.VMEM), pl.BlockSpec(memory_space=pltpu.VMEM)),
        scratch_shapes=[
            pltpu.VMEM((NZ, MATS, ROWS, CHUNK), grads.dtype),
            pltpu.VMEM((NZ, MATS, ROWS, CHUNK), f32),
            pltpu.VMEM((MATS, 2, blocks, ROWS, BLOCK), f32),
            pltpu.VMEM((MATS, blocks, ROWS, BLOCK), f32),
            pltpu.VMEM((NZ, 2, ROWS, BLOCK), f32),
            pltpu.VMEM((NZ, 2, ROWS, BLOCK), f32),
            pltpu.VMEM((NZ, NX, ROWS, BLOCK), f32),
            pltpu.VMEM((NZ, NX, ROWS, BLOCK), f32),
            pltpu.VMEM((NZ, NX, ROWS, BLOCK), f32),
            pltpu.VMEM((NZ, NX, ROWS, BLOCK), f32),
            pltpu.VMEM((NZ, NX, RANK, BLOCK), f32),
            pltpu.VMEM((ROWS, RANK), f32),
            pltpu.VMEM((2, ROWS // 2, RANK), f32),
            pltpu.VMEM((ROWS // 2, RANK), f32),
            pltpu.VMEM((NZ, NX, 2, 8, BLOCK), f32),
            pltpu.VMEM((NZ, RANK, BLOCK), f32),
            pltpu.VMEM((NZ, NX, ROWS, BLOCK), f32),
            pltpu.VMEM((2, MATS, blocks + 2, ROWS, BLOCK), f32),
            dma((2, 8)), dma,
            dma((8,)), dma((8,)),
            dma((2, 8)), dma((2, 8)),
            dma((2, 8)), dma((2, 8)),
            dma((NZ, NX)), dma((NZ, NX)),
            dma((NZ,)), dma((NZ,)),
            dma((NZ, NX)), dma((NZ, NX)),
            pltpu.SemaphoreType.REGULAR, pltpu.SemaphoreType.REGULAR((2, 4)),
            dma, dma,
            dma((NZ,)), dma((NZ,)),
            dma((NZ, NX)), dma((NZ, NX)),
            dma, dma,
            dma((NZ, NX)), dma((NZ, NX)),
            dma((2, 9)), dma((2, 9)),
            dma((2, 9)), dma((2, 9)),
            dma((MATS, 9)), dma((MATS, 9)),
        ],
        name="powersgd",
        compiler_params=pltpu.CompilerParams(
            collective_id=0, has_side_effects=True, vmem_limit_bytes=46 << 20
        ),
    )(*(pltpu.with_memory_space_constraint(v, pltpu.HBM) for v in (grads, errors, jnp.swapaxes(q_prev, 1, 2))))
    errors_new, q_new = pl.pallas_call(
        store,
        out_shape=(jax.ShapeDtypeStruct(errors_new.shape, f32), jax.ShapeDtypeStruct(q_new.shape, f32)),
        in_specs=[pl.BlockSpec(memory_space=pltpu.VMEM)] * 2,
        out_specs=(pl.BlockSpec(memory_space=pl.ANY),) * 2,
        scratch_shapes=[dma((MATS + 1,))],
        name="store",
        compiler_params=pltpu.CompilerParams(vmem_limit_bytes=16 << 20),
    )(*(pltpu.with_memory_space_constraint(v, pltpu.VMEM) for v in (errors_new, q_new)))
    return jnp.swapaxes(q_new, 1, 2), errors_new


def solution(mesh):
    return jax.shard_map(
        body,
        mesh=mesh,
        in_specs=(P("dp", None, "rows", None), P("dp", None, "rows", None), P(None, "rows", None)),
        out_specs=(P(None, "rows", None), P("dp", None, "rows", None)),
        check_vma=False,
    )
```

```python
import jax
import jax.numpy as jnp
from jax import lax
from jax.experimental import pallas as pl
from jax.experimental.pallas import tpu as pltpu
from jax.sharding import PartitionSpec as P

MESH = pl.DeviceIdType.MESH
HIGHEST = lax.Precision.HIGHEST
NX, NY, NZ = 4, 4, 8
MATS, ROWS, RANK, GROUPS = 4, 32, 64, 8
BLOCK = 128
CHUNK = NX * 2 * BLOCK
DAMP = 0.0001

NN = (((1,), (0,)), ((), ()))
NT = (((1,), (1,)), ((), ()))

ORDER = (0, 1, 7, 2, 6, 3, 5, 4)
IN_ORDER = (4, 3, 5, 2, 6, 1, 7, 0)
ONWARD = {0: (1, 7), 1: (2,), 2: (3,), 3: (4,), 4: (), 5: (), 6: (5,), 7: (6,)}
ONWARD_FAR = {2: (3,), 3: (4,), 6: (5,)}
PEERS = tuple((t, dx) for t in ORDER for dx in range(NX) if (t, dx) != (0, 0))


def dot(a, b, dims=NN):
    return lax.dot_general(a, b, dims, precision=HIGHEST, preferred_element_type=jnp.float32)


def inverse_factor(gram):
    n = RANK
    row = lax.broadcasted_iota(jnp.int32, (n, n), 0)
    col = lax.broadcasted_iota(jnp.int32, (n, n), 1)
    eye = jnp.where(row == col, 1.0, 0.0).astype(jnp.float32)
    trace = jnp.sum(gram * eye, axis=(0, 1), keepdims=True)
    full = jnp.concatenate([gram + (DAMP / n) * trace * eye, eye], axis=1)
    strips = [full[8 * i : 8 * i + 8] for i in range(n // 8)]
    sub = lax.broadcasted_iota(jnp.int32, (8, 2 * n), 0)
    scales = []
    for b in range(n // 8):
        live = range(b, n // 8)
        cols = {
            (i, j): jnp.broadcast_to(strips[i][:, 8 * b + j : 8 * b + j + 1], (8, 2 * n))
            for i in live
            for j in range(8)
        }
        scale = jnp.zeros((8, 2 * n), jnp.float32)
        for j in range(8):
            pivot = jnp.broadcast_to(cols[b, j][j : j + 1], (8, 2 * n))
            inv = 1.0 / pivot
            scale = jnp.where(sub == j, lax.rsqrt(pivot), scale)
            factor = {i: cols[i, j] for i in live}
            factor[b] = jnp.where(sub > j, factor[b], 0.0)
            lead = jnp.broadcast_to(strips[b][j : j + 1], (8, 2 * n)) * inv
            heads = {q: jnp.broadcast_to(cols[b, q][j : j + 1], (8, 2 * n)) * inv for q in range(j + 1, 8)}
            for i in live:
                strips[i] = strips[i] - factor[i] * lead
                for q in range(j + 1, 8):
                    cols[i, q] = cols[i, q] - factor[i] * heads[q]
        scales.append(scale)
    done = jnp.concatenate([s * c for s, c in zip(strips, scales)], axis=0)
    return done[:, n:]


def kernel(
    grads, errors, q_prev, q_out, e_out,
    g_in, e_in, merged, summed, pass_up, pass_dn, fin_up, fin_dn, mean, meant, q_all,
    acc, half_out, half_in, left, v_all, block_out, approx,
    ld_sem, q_sem, core_s, core_r, pass_s, pass_r, fin_s, fin_r, m_s, m_r, qz_s, qz_r, qx_s, qx_r, x_known, z_known,
    h_s, h_r, v_s, v_r, l_s, l_r, lc_s, lc_r, a_s, a_r, y_s, y_r, rel_s, rel_r, ac_s, ac_r,
):
    d, r = lax.axis_index("dp"), lax.axis_index("rows")
    y, k = d // 2, d % 2
    z, x = r // NX, r % NX
    other = 1 - k
    y_up, y_dn, y_far = (y + 1) % NY, (y + 3) % NY, (y + 2) % NY
    partner = (y * 2 + other, r)
    up = (y_up * 2 + k, r)
    down = (y_dn * 2 + k, r)

    def peer(t, dx):
        return (d, ((z + t) % NZ) * NX + (x + dx) % NX)

    def zat(t):
        return (z + t) % NZ

    def xat(dx):
        return (x + dx) % NX

    def ring(buf, ss, rs, copies, t, onward=ONWARD):
        here = buf((z + NZ - t) % NZ)
        for u in onward.get(t, ()):
            copies[u] = send(here, here, ss.at[u], rs.at[u], peer(1 if u <= 4 else 7, 0))

    sends = []

    def flush():
        while sends:
            sends.pop(0).wait_send()

    def send(src, dst, ss, rs, to):
        copy = pltpu.make_async_remote_copy(
            src_ref=src, dst_ref=dst, send_sem=ss, recv_sem=rs, device_id=to, device_id_type=MESH
        )
        copy.start()
        sends.append(copy)
        return copy

    loads = {}
    q_load = pltpu.make_async_copy(
        q_prev.at[y, :, pl.ds(pl.multiple_of(k * BLOCK, BLOCK), BLOCK)], q_all.at[z, x], q_sem
    )
    q_load.start()
    for n, t in enumerate(IN_ORDER):
        at = pl.ds(pl.multiple_of(zat(t) * CHUNK, CHUNK), CHUNK)
        loads[n] = (
            pltpu.make_async_copy(grads.at[0, :, :, at], g_in.at[zat(t)], ld_sem.at[0, n]),
            pltpu.make_async_copy(errors.at[0, :, :, at], e_in.at[zat(t)], ld_sem.at[1, n]),
        )
        for load in loads[n]:
            load.start()

    barrier = pltpu.get_barrier_semaphore()
    near = [partner, up, down, peer(1, 0), peer(7, 0), peer(0, 1), peer(0, 3)]
    for to in near:
        pl.semaphore_signal(barrier, inc=1, device_id=to, device_id_type=MESH)
    core, passes, finals, q_z, q_x = {}, {}, {}, {}, {}

    def four(c):
        return pl.ds(pl.multiple_of(c * NX, NX), NX)

    def merge(n):
        c = zat(IN_ORDER[n])
        for load in loads[n]:
            load.wait()

        def one(m, _):
            for j in range(2 * NX):
                cols = slice(j * BLOCK, (j + 1) * BLOCK)
                merged[m, j % 2, c * NX + j // 2] = g_in[c, m, :, cols].astype(jnp.float32) + e_in[c, m, :, cols]
            return 0

        lax.fori_loop(0, MATS, one, 0)

    def swap_cores(n):
        c = zat(IN_ORDER[n])
        core[n] = send(merged.at[:, other, four(c)], summed.at[:, four(c)], core_s.at[n], core_r.at[n], partner)

    def pair_sum(n):
        c = zat(IN_ORDER[n])
        core[n].wait_recv()

        def one(m, _):
            for j in range(NX):
                summed[m, c * NX + j] += merged[m, k, c * NX + j]
            return 0

        lax.fori_loop(0, MATS, one, 0)
        passes[n] = (
            send(summed.at[y_far, pl.ds(c * NX, 2)], pass_up.at[c], pass_s.at[0, n], pass_r.at[0, n], up),
            send(summed.at[y_far, pl.ds(c * NX + 2, 2)], pass_dn.at[c], pass_s.at[1, n], pass_r.at[1, n], down),
        )

    def pass_on(n):
        c = zat(IN_ORDER[n])
        for copy in passes[n]:
            copy.wait_recv()
        for j in range(2):
            summed[y_up, c * NX + j] += pass_up[c, j]
            summed[y_dn, c * NX + 2 + j] += pass_dn[c, j]
        finals[n] = (
            send(summed.at[y_up, four(c)], fin_up.at[c], fin_s.at[0, n], fin_r.at[0, n], up),
            send(summed.at[y_dn, four(c)], fin_dn.at[c], fin_s.at[1, n], fin_r.at[1, n], down),
        )

    mean_sent = {}

    def total(n):
        c = zat(IN_ORDER[n])
        for copy in finals[n]:
            copy.wait_recv()
        for j in range(NX):
            mean[c, j] = summed[y, c * NX + j] + fin_up[c, j] + fin_dn[c, j]

    def scatter(n):
        t = IN_ORDER[n]
        c = zat(t)
        for dx in range(NX):
            if (t, dx) == (0, 0):
                meant[z, x] = mean[z, x]
            else:
                mean_sent[t, dx] = send(
                    mean.at[c, xat(dx)], meant.at[z, x], m_s.at[t, dx], m_r.at[t, dx], peer(t, dx)
                )

    def hello(n):
        if n == 1:
            pl.semaphore_wait(x_known, 1)
        elif n == 5:
            pl.semaphore_wait(z_known.at[0, 3], 1)
        elif n > 1:
            for way in range(2):
                pl.semaphore_wait(z_known.at[way, n - 2], 1)
        if n == 0:
            pl.semaphore_signal(x_known, inc=1, device_id=peer(0, 1), device_id_type=MESH)
        elif n < 5:
            for way in range(2 if n < 4 else 1):
                to = peer((1, 7)[way], 0)
                pl.semaphore_signal(z_known.at[way, n - 1], inc=1, device_id=to, device_id_type=MESH)

    def spread_q(t):
        if t > 0:
            q_z[t].wait_recv()
        ring(lambda c: q_all.at[c, x], qz_s, qz_r, q_z, t)
        here = q_all.at[(z + NZ - t) % NZ, x]
        for dx in (1, 3):
            q_x[t, dx] = send(here, here, qx_s.at[t, dx], qx_r.at[t, dx], peer(0, dx))

    def relay_q(t):
        for dx in (1, 3):
            q_x[t, dx].wait_recv()
        dx = 1 if t < 4 else 3
        here = q_all.at[(z + NZ - t) % NZ, xat(NX - dx)]
        q_x[t, 2] = send(here, here, qx_s.at[t, 2], qx_r.at[t, 2], peer(0, dx))

    def project(n):
        t = IN_ORDER[n]
        c = zat(t)
        q_x[(NZ - t) % NZ, 2].wait_recv()
        part = dot(mean[c, 0], q_all[c, 0], NT)
        for j in range(1, NX):
            part = part + dot(mean[c, j], q_all[c, j], NT)
        acc[...] += part

    steps = len(IN_ORDER)
    merge(0)
    pl.semaphore_wait(barrier, len(near))
    swap_cores(0)
    q_load.wait()
    acc[...] = jnp.zeros_like(acc)
    plan = [
        (hello, 0), (merge, 1), (swap_cores, 1), (spread_q, 0), (merge, 2), (swap_cores, 2), (pair_sum, 0),
        (hello, 1), (merge, 3), (swap_cores, 3), (pair_sum, 1), (merge, 4), (swap_cores, 4), (pair_sum, 2),
        (merge, 5), (swap_cores, 5), (hello, 2), (pair_sum, 3), (merge, 6), (swap_cores, 6), (pair_sum, 4),
        (merge, 7), (swap_cores, 7), (pair_sum, 5), (hello, 3), (pair_sum, 6), (pair_sum, 7), (pass_on, 0),
        (spread_q, 1), (spread_q, 7), (pass_on, 1), (hello, 4), (pass_on, 2), (relay_q, 0), (pass_on, 3),
        (spread_q, 2), (spread_q, 6), (pass_on, 4), (relay_q, 1), (relay_q, 7), (hello, 5), (pass_on, 5),
        (pass_on, 6), (pass_on, 7), (total, 0), (scatter, 0), (spread_q, 3), (spread_q, 5), (total, 1),
        (scatter, 1), (relay_q, 2), (relay_q, 6), (total, 2), (scatter, 2), (spread_q, 4), (total, 3),
        (scatter, 3), (relay_q, 3), (relay_q, 5), (total, 4), (scatter, 4), (project, 4), (project, 3),
        (relay_q, 4), (total, 5), (scatter, 5), (project, 5), (project, 1), (project, 2), (total, 6),
        (scatter, 6), (project, 6), (project, 0), (total, 7), (scatter, 7), (project, 7),
    ]
    for step, n in plan:
        step(n)

    half_out[0] = acc[:16]
    half_out[1] = acc[16:]
    swap = send(half_out.at[other], half_in, h_s, h_r, partner)
    swap.wait_recv()
    mine = (half_out[k] + half_in[...]) * (1.0 / GROUPS)
    left[z, x, k] = jnp.concatenate([mine[:8], mine[8:]], axis=1)
    spread = [
        send(left.at[z, x, k], left.at[z, x, k], l_s.at[t, dx], l_r.at[t, dx], peer(t, dx))
        for t, dx in reversed(PEERS)
    ]
    flush()
    for copy in spread:
        copy.wait_recv()
    cross = send(left.at[:, :, k], left.at[:, :, k], lc_s, lc_r, partner)

    def rows_of(i, j):
        return pl.ds(pl.multiple_of(16 * i + 8 * j, 8), 8)

    def gram_of(i):
        part = left[:, :, i].reshape(NZ * NX * 8, BLOCK)
        turned = jnp.transpose(part)
        return turned, dot(turned, part)

    def projection(i, turned):
        prod = [dot(turned, meant[:, :, rows_of(i, j)].reshape(NZ * NX * 8, BLOCK)) for j in range(2)]
        return prod[0][:RANK] + prod[1][RANK:]

    turned, square = gram_of(k)
    cross.wait_recv()
    turned_other, more = gram_of(other)
    square = square + more
    for copy in mean_sent.values():
        copy.wait_recv()
    v_all[z] = projection(k, turned) + projection(other, turned_other)
    v_sent = {t: send(v_all.at[z], v_all.at[z], v_s.at[t], v_r.at[t], peer(t, 0)) for t in (1, 7, 2, 6)}
    inv = inverse_factor(square[:RANK, :RANK] + square[RANK:, RANK:])
    rows = left[z].reshape(NX * 2 * 8, BLOCK)
    ortho = jnp.concatenate([dot(rows[:, :RANK], inv, NT), dot(rows[:, RANK:], inv, NT)], axis=0)
    blocks, direct, relay, crossed = {}, {}, {}, {}
    early = list(sends)
    sends.clear()

    def expand(n):
        t = ORDER[n]
        c = (z + NZ - t) % NZ
        if n > 0:
            v_sent[t].wait_recv()
        ring(lambda c: v_all.at[c], v_s, v_r, v_sent, t, ONWARD_FAR)
        q_part = dot(inv, v_all[c]) * (1.0 / GROUPS)
        if n == 0:
            approx[k, y, 32] = q_part[:32]
            approx[k, y, 33] = q_part[32:]
        got = dot(ortho, q_part).reshape(2, NX, 2, 8, BLOCK)
        for i in range(2):
            for j in range(2):
                block_out[c, :, rows_of(i, j)] = got[j, :, i]
        for dx in range(1, NX):
            blocks[n, dx] = send(
                block_out.at[c, xat(dx)], approx.at[k, y, c * NX + x], a_s.at[t, dx], a_r.at[t, dx], peer(0, dx)
            )
        approx[k, y, c * NX + x] = block_out[c, x]


    def places(n):
        if n == steps:
            return pl.ds(32, 2), pl.ds(32, 1), pl.ds(33, 1)
        c = (z + NZ - ORDER[n]) % NZ
        return four(c), pl.ds(c * NX, 2), pl.ds(c * NX + 2, 2)

    def share(n):
        if n < steps:
            for dx in range(1, NX):
                blocks[n, dx].wait_recv()
        at = places(n)[0]
        here = approx.at[k, y, at]
        direct[n] = (
            send(here, here, y_s.at[0, n], y_r.at[0, n], up),
            send(here, here, y_s.at[1, n], y_r.at[1, n], down),
        )

    def cross_over(n, m, slot):
        here = approx.at[k, m, places(n)[0]]
        crossed[n, slot] = send(here, here, ac_s.at[slot, n], ac_r.at[slot, n], partner)

    def pass_along(n):
        _, first, second = places(n)
        for copy in direct[n]:
            copy.wait_recv()
        from_dn, from_up = approx.at[k, y_dn, first], approx.at[k, y_up, second]
        relay[n] = (
            send(from_dn, from_dn, rel_s.at[0, n], rel_r.at[0, n], up),
            send(from_up, from_up, rel_s.at[1, n], rel_r.at[1, n], down),
        )
        for slot, m in enumerate((y, y_up, y_dn)):
            cross_over(n, m, slot)

    def over(n):
        for copy in relay[n]:
            copy.wait_recv()
        cross_over(n, y_far, 3)

    def tidy(n):
        for copy in early:
            copy.wait_send()
        early.clear()
        for _ in range(n):
            sends.pop(0).wait_send()

    def finish(n):
        for slot in range(MATS):
            crossed[n, slot].wait_recv()
        if n == steps:
            for m in range(MATS):
                for h in range(2):
                    q_out[m, :, h * BLOCK : (h + 1) * BLOCK] = approx[h, m, 32:34].reshape(RANK, BLOCK)
            return
        c = (z + NZ - ORDER[n]) % NZ

        def one(m, _):
            for j in range(2 * NX):
                b = c * NX + j // 2
                at = pl.ds(pl.multiple_of(c * CHUNK + j * BLOCK, BLOCK), BLOCK)
                e_out[0, m, :, at] = merged[m, j % 2, b] - approx[j % 2, m, b]
            return 0

        lax.fori_loop(0, MATS, one, 0)

    Q = steps
    plan = [
        (expand, 0), (share, Q), (expand, 1), (expand, 2), (share, 0), (expand, 3), (expand, 4), (share, 1),
        (share, 2), (pass_along, Q), (pass_along, 0), (expand, 5), (expand, 6), (share, 3), (share, 4),
        (pass_along, 1), (pass_along, 2), (expand, 7), (over, Q), (over, 0), (share, 5), (share, 6),
        (pass_along, 3), (pass_along, 4), (over, 1), (over, 2), (share, 7), (finish, Q), (finish, 0),
        (pass_along, 5), (pass_along, 6), (over, 3), (over, 4), (finish, 1), (finish, 2), (pass_along, 7),
        (over, 5), (over, 6), (finish, 3), (finish, 4), (tidy, 80), (over, 7), (finish, 5), (finish, 6), (finish, 7),
    ]
    for step, n in plan:
        step(n)
    flush()


def store(e_in, q_in, e_out, q_out, sem):
    copies = [pltpu.make_async_copy(e_in.at[:, m], e_out.at[:, m], sem.at[m]) for m in range(MATS)]
    copies.append(pltpu.make_async_copy(q_in, q_out, sem.at[MATS]))
    for copy in copies:
        copy.start()
    for copy in copies:
        copy.wait()


def body(grads, errors, q_prev):
    f32 = jnp.float32
    dma = pltpu.SemaphoreType.DMA
    blocks = NZ * NX
    q_new, errors_new = pl.pallas_call(
        kernel,
        out_shape=(
            jax.ShapeDtypeStruct((MATS, RANK, 2 * BLOCK), f32),
            jax.ShapeDtypeStruct(errors.shape, f32),
        ),
        in_specs=[pl.BlockSpec(memory_space=pltpu.HBM)] * 3,
        out_specs=(pl.BlockSpec(memory_space=pltpu.VMEM), pl.BlockSpec(memory_space=pltpu.VMEM)),
        scratch_shapes=[
            pltpu.VMEM((NZ, MATS, ROWS, CHUNK), grads.dtype),
            pltpu.VMEM((NZ, MATS, ROWS, CHUNK), f32),
            pltpu.VMEM((MATS, 2, blocks, ROWS, BLOCK), f32),
            pltpu.VMEM((MATS, blocks, ROWS, BLOCK), f32),
            pltpu.VMEM((NZ, 2, ROWS, BLOCK), f32),
            pltpu.VMEM((NZ, 2, ROWS, BLOCK), f32),
            pltpu.VMEM((NZ, NX, ROWS, BLOCK), f32),
            pltpu.VMEM((NZ, NX, ROWS, BLOCK), f32),
            pltpu.VMEM((NZ, NX, ROWS, BLOCK), f32),
            pltpu.VMEM((NZ, NX, ROWS, BLOCK), f32),
            pltpu.VMEM((NZ, NX, RANK, BLOCK), f32),
            pltpu.VMEM((ROWS, RANK), f32),
            pltpu.VMEM((2, ROWS // 2, RANK), f32),
            pltpu.VMEM((ROWS // 2, RANK), f32),
            pltpu.VMEM((NZ, NX, 2, 8, BLOCK), f32),
            pltpu.VMEM((NZ, RANK, BLOCK), f32),
            pltpu.VMEM((NZ, NX, ROWS, BLOCK), f32),
            pltpu.VMEM((2, MATS, blocks + 2, ROWS, BLOCK), f32),
            dma((2, 8)), dma,
            dma((8,)), dma((8,)),
            dma((2, 8)), dma((2, 8)),
            dma((2, 8)), dma((2, 8)),
            dma((NZ, NX)), dma((NZ, NX)),
            dma((NZ,)), dma((NZ,)),
            dma((NZ, NX)), dma((NZ, NX)),
            pltpu.SemaphoreType.REGULAR, pltpu.SemaphoreType.REGULAR((2, 4)),
            dma, dma,
            dma((NZ,)), dma((NZ,)),
            dma((NZ, NX)), dma((NZ, NX)),
            dma, dma,
            dma((NZ, NX)), dma((NZ, NX)),
            dma((2, 9)), dma((2, 9)),
            dma((2, 9)), dma((2, 9)),
            dma((MATS, 9)), dma((MATS, 9)),
        ],
        name="powersgd",
        compiler_params=pltpu.CompilerParams(
            collective_id=0, has_side_effects=True, vmem_limit_bytes=46 << 20
        ),
    )(*(pltpu.with_memory_space_constraint(v, pltpu.HBM) for v in (grads, errors, jnp.swapaxes(q_prev, 1, 2))))
    errors_new, q_new = pl.pallas_call(
        store,
        out_shape=(jax.ShapeDtypeStruct(errors_new.shape, f32), jax.ShapeDtypeStruct(q_new.shape, f32)),
        in_specs=[pl.BlockSpec(memory_space=pltpu.VMEM)] * 2,
        out_specs=(pl.BlockSpec(memory_space=pl.ANY),) * 2,
        scratch_shapes=[dma((MATS + 1,))],
        name="store",
        compiler_params=pltpu.CompilerParams(vmem_limit_bytes=16 << 20),
    )(*(pltpu.with_memory_space_constraint(v, pltpu.VMEM) for v in (errors_new, q_new)))
    return jnp.swapaxes(q_new, 1, 2), errors_new


def solution(mesh):
    return jax.shard_map(
        body,
        mesh=mesh,
        in_specs=(P("dp", None, "rows", None), P("dp", None, "rows", None), P(None, "rows", None)),
        out_specs=(P(None, "rows", None), P("dp", None, "rows", None)),
        check_vma=False,
    )
```
